256 devices in a mesh: seq: 16 (over z, y_lo), row: 2 (over y_hi), col: 8 (over x, core).
Axes of the slice: x: 4, y: 4 (y_hi: 2, y_lo: 2; y = y_hi * 2 + y_lo), z: 8, core: 2. Of those that a mesh axis runs over, the one named last changes fastest.
Arguments:
- tokens: bfloat16 [8192, 4096], P(('seq', 'row'), 'col'), may hold values from -20 to 20
- w_query: bfloat16 [4096, 2048], P('row', 'col'), may hold values from -1 to 1
- w_key: bfloat16 [4096, 2048], P('row', 'col'), may hold values from -1 to 1
- w_value: bfloat16 [4096, 2048], P('row', 'col'), may hold values from -0.09375 to 0.09375
- w_out: bfloat16 [2048, 4096], P('row', 'col'), may hold values from -0.125 to 0.125
Outputs:
- mixed: bfloat16 [8192, 4096], P(('seq', 'row'), 'col')
The draws below stay inside these ranges and needn't reach their ends.
All inputs are finite; a program needn't handle non-finite values.
Results may differ from the reference program's by a relative error of at most 0.01125.
Values may be sent and summed in bfloat16 or wider, within the bound.
A program may use at most 64 MiB of HBM per device.

```python
import jax
import jax.numpy as jnp
from jax import lax

D = 4096
HEADS = 32
HEAD_DIM = 64
HW = 2048
SEQ_LEN = 8192


def draw_w_query(key, part):
    key = jax.random.fold_in(key, 11)
    own = jax.random.normal(key, (D, HW), jnp.float32) * D ** (-0.5)
    matrix = own
    return matrix.astype(jnp.bfloat16)


def draw_w_key(key, part):
    key = jax.random.fold_in(key, 12)
    own = jax.random.normal(key, (D, HW), jnp.float32) * D ** (-0.5)
    matrix = own
    return matrix.astype(jnp.bfloat16)


def draw_tokens(key, part):
    key = jax.random.fold_in(key, 13)
    first = jax.random.fold_in(key, 0)
    base = jnp.clip(jax.random.normal(first, (SEQ_LEN, D), jnp.float32), -6.0, 6.0)
    result = base
    return result.astype(jnp.bfloat16)


def steps_of(rng, dims, pieces, smallest, top_value):
    level, own = 1.0, jax.random.fold_in(rng, 6)
    for axis_at, parts in pieces:
        draws = jnp.exp(jax.random.uniform(jax.random.fold_in(own, axis_at), (parts,), jnp.float32, smallest / len(pieces), top_value / len(pieces)))
        level = level * jnp.repeat(draws, dims[axis_at] // parts).reshape([-1 if axis == axis_at else 1 for axis in range(len(dims))])
    return level


def centred(rng, shape, spread, reach, cuts=(), dtype=jnp.bfloat16):
    entries = jax.random.normal(rng, shape, jnp.float32) * spread
    if len(cuts) > 0:
        entries = steps_of(rng, shape, cuts, -0.22, 0.18) * entries
    return jnp.clip(entries, min=-reach, max=reach).astype(dtype)


def setup_inputs(seed: int = 0) -> dict:
    arg_keys = jax.random.split(jax.random.key(seed), 6)
    return {
        "tokens": draw_tokens(jax.random.fold_in(arg_keys[5], 71), 0),
        "w_query": draw_w_query(jax.random.fold_in(arg_keys[5], 71), 0),
        "w_key": draw_w_key(jax.random.fold_in(arg_keys[5], 71), 0),
        "w_value": centred(arg_keys[3], (D, HW), D ** -0.5, 0.09375, ((0, 2), (1, 8))),
        "w_out": centred(arg_keys[4], (HW, D), HW ** -0.5, 0.125, ((0, 2), (1, 8))),
    }


def one_head(operands):
    query_h, keys_h, values_h = operands
    block = min(1024, SEQ_LEN)
    scale = 1.0 / (HEAD_DIM ** 0.5)
    query_blocks = query_h.reshape(SEQ_LEN // block, block, HEAD_DIM)

    def per_block(query_b):
        scores = jnp.dot(query_b.astype(jnp.float32), keys_h.astype(jnp.float32).T) * scale
        top = jnp.max(scores, axis=1, keepdims=True)
        expo = jnp.exp(scores - top)
        total = jnp.sum(expo, axis=1, keepdims=True)
        weights = expo.astype(jnp.bfloat16)
        return jnp.dot(weights, values_h, preferred_element_type=jnp.float32) / total

    return lax.map(per_block, query_blocks).reshape(SEQ_LEN, HEAD_DIM)


def reference(tokens, w_query, w_key, w_value, w_out):
    query = jnp.dot(tokens, w_query, preferred_element_type=jnp.float32).astype(jnp.bfloat16)
    keys = jnp.dot(tokens, w_key, preferred_element_type=jnp.float32).astype(jnp.bfloat16)
    values = jnp.dot(tokens, w_value, preferred_element_type=jnp.float32).astype(jnp.bfloat16)

    def split_heads(matrix):
        return matrix.reshape(SEQ_LEN, HEADS, HEAD_DIM).transpose(1, 0, 2)

    attended = lax.map(one_head, (split_heads(query), split_heads(keys), split_heads(values)))
    attended = attended.transpose(1, 0, 2).reshape(SEQ_LEN, HW).astype(jnp.bfloat16)
    return jnp.dot(attended, w_out, preferred_element_type=jnp.float32).astype(jnp.bfloat16)
```

```python
import math

import jax
import jax.numpy as jnp
from jax import lax
from jax.experimental import pallas as pl
from jax.experimental.pallas import tpu as pltpu
from jax.sharding import PartitionSpec as P

HEAD_DIM = 64
NCH = 4
F32 = jnp.float32
BF16 = jnp.bfloat16


def dot_t(a, b):
    return lax.dot_general(a, b, (((1,), (1,)), ((), ())), preferred_element_type=F32)


def dot(a, b):
    return jnp.dot(a, b, preferred_element_type=F32)


def kernel(
    tok, wq, wk, wv, wo, out,
    tokbuf, wbuf, wobuf, pf, cs, cr, kvo, kvb, qof, qs, qr, qb, mst, acc, ao, att, lhs, gs, gr,
    wsem, locsem, ts, tr, psem, csem, crsem, ksem, krsem, qsem, qrsem, rsem, rrsem, fsem, asem, arsem, gsem, grsem,
):
    seq, yh, col = lax.axis_index("seq"), lax.axis_index("row"), lax.axis_index("col")
    z, yl = seq // 2, seq % 2
    x, k = col // 2, col % 2
    xp = x % 2
    hx = x // 2
    y = yh * 2 + yl
    src = 1 - (hx - yh) * (hx - yh)
    is_src, is_sink = src == 1, src == 0

    def dev(seq=seq, row=yh, col=col):
        return {"seq": seq, "row": row, "col": col}

    sib = dev(col=x * 2 + 1 - k)
    xsw = dev(col=(x + 1 - 2 * xp) * 2 + k)
    xop = dev(col=(3 - x) * 2 + k)
    part = dev(seq=z * 2 + 1 - yl, row=1 - yh)
    ysw = dev(seq=z * 2 + 1 - yl)
    yac = dev(row=1 - yh)
    zr = dev(seq=((z + 1) % 8) * 2 + yl)
    zl = dev(seq=((z + 7) % 8) * 2 + yl)

    def rc(s, d, ss, rs, to):
        return pltpu.make_async_remote_copy(
            src_ref=s, dst_ref=d, send_sem=ss, recv_sem=rs, device_id=to,
            device_id_type=pl.DeviceIdType.MESH,
        )

    wloads = [
        pltpu.make_async_copy(w, wbuf.at[i], wsem.at[i]) for i, w in enumerate((wq, wk, wv))
    ]
    wloads.append(pltpu.make_async_copy(wo, wobuf, wsem.at[3]))
    for w in wloads:
        w.start()
    own_f = xp * 2 + k
    a0, a1 = yh, 1 - yh
    tload = pltpu.make_async_copy(tok, tokbuf.at[a0, own_f], locsem)

    @pl.when(is_src)
    def _():
        tload.start()

    barrier = pltpu.get_barrier_semaphore()
    for to in (sib, xsw, xop, part, ysw, yac, zr, zl):
        pl.semaphore_signal(barrier, inc=1, device_id=to, device_id_type=pl.DeviceIdType.MESH)
    pl.semaphore_wait(barrier, 8)

    xpp = src * xp + (1 - src) * (1 - xp)
    fp, fs = xpp * 2 + k, (1 - xpp) * 2 + k
    fps, fss = xpp * 2 + 1 - k, (1 - xpp) * 2 + 1 - k
    rows = 256 // NCH

    def tchunk(c):
        return tok.at[pl.ds(c * rows, rows), :]

    def tslot(a, f, c):
        return tokbuf.at[a, f, pl.ds(c * rows, rows), :]

    def tcopy(s, a, f, kind, c, to):
        return rc(s, tslot(a, f, c), ts.at[a, kind, c], tr.at[a, f, c], to)

    def twait(a, f, c):
        tcopy(tslot(a, f, c), a, f, 0, c, sib).wait_recv()

    def tprim(a, c, s):
        tcopy(s, a, fp, 0, c, xsw).start()

        @pl.when(is_src)
        def _():
            tcopy(s, a, fp, 2, c, xop).start()

        tcopy(s, a, fp, 1, c, sib).start()

    def tsec(a, c):
        tcopy(tslot(a, fs, c), a, fs, 3, c, sib).start()

    def pcopy(c):
        return rc(tchunk(c), tslot(a0, own_f, c), psem.at[c], tr.at[a0, own_f, c], part)

    @pl.when(is_src)
    def _():
        for c in range(NCH):
            tprim(a0, c, tchunk(c))

    @pl.when(is_sink)
    def _():
        for c in range(NCH):
            pcopy(c).start()

    for i in range(NCH + 1):
        if i < NCH:
            @pl.when(is_sink)
            def _():
                twait(a0, fp, i)
                tprim(a0, i, tslot(a0, fp, i))
        if i >= 1:
            twait(a0, fs, i - 1)
            tsec(a0, i - 1)

    @pl.when(is_src)
    def _():
        for c in range(NCH):
            twait(a1, fp, c)
            tprim(a1, c, tslot(a1, fp, c))
        tload.wait()

    for w in wloads:
        w.wait()

    def ccopy(a, i):
        return rc(cs.at[a, i], cr.at[a, i], csem.at[a, i], crsem.at[a, i], part)

    def project(a):
        for i in (1, 2, 0):
            full = dot(tokbuf[a, 0], wbuf[i, 0:512, :])
            for f in range(1, 4):
                full += dot(tokbuf[a, f], wbuf[i, f * 512 : (f + 1) * 512, :])
            lo, hi = full[:, :128], full[:, 128:]
            cs[a, i] = jnp.where(yh == 0, hi, lo).astype(BF16)
            ccopy(a, i).start()
            pf[a, i] = jnp.where(yh == 0, lo, hi)

    for c in range(NCH):
        twait(a0, fps, c)
        twait(a0, fss, c)
    project(a0)

    for i in range(NCH + 1):
        if i < NCH:
            @pl.when(is_sink)
            def _():
                twait(a1, fp, i)
                tprim(a1, i, tslot(a1, fp, i))
        if i >= 1:
            twait(a1, fs, i - 1)
            tsec(a1, i - 1)
    for c in range(NCH):
        twait(a1, fps, c)
        twait(a1, fss, c)
    project(a1)

    low = lax.broadcasted_iota(jnp.int32, (256, 128), 1) < 64
    qscale = math.log2(math.e) / HEAD_DIM**0.5

    def half(a):
        return pl.ds(pl.multiple_of(a * 256, 256), 256)

    def kcopy(a):
        return rc(kvo.at[a], kvb.at[z, 1, half(a), :], ksem.at[a], krsem.at[a], ysw)

    for a in (a0, a1):
        ccopy(a, 1).wait_recv()
        ccopy(a, 2).wait_recv()
        ks = pf[a, 1] + cr[a, 1].astype(F32)
        vs = pf[a, 2] + cr[a, 2].astype(F32)
        kv0 = jnp.where(low, ks, pltpu.roll(vs, 64, 1))
        kv1 = jnp.where(low, pltpu.roll(ks, 64, 1), vs)
        kvo[a] = jnp.where(yl == 0, kv1, kv0).astype(BF16)
        kcopy(a).start()
        kvb[z, 0, half(a), :] = jnp.where(yl == 0, kv0, kv1).astype(BF16)

    def slots(i):
        t = i + 1
        d = (t + 1) // 2
        g_r = (t + 1) % 2
        ends = t // 7 + (7 - t) // 7
        g_l = g_r + ends * (1 - 2 * g_r)
        return (z - d + 8) % 8, g_r, (z + d) % 8, g_l

    def ring(way, i, zs, g):
        ref = kvb.at[zs, g]
        return rc(ref, ref, rsem.at[way, i], rrsem.at[way, i], (zr, zl)[way])

    for way in (0, 1):
        ring(way, 0, z, 0).start()

    for a in (a0, a1):
        ccopy(a, 0).wait_recv()
        q = (pf[a, 0] + cr[a, 0].astype(F32)) * qscale
        qx = pltpu.roll(q, 64, 1)
        qb[half(a), :] = jnp.where(low, jnp.where(yl == 0, q, qx), 0.0).astype(BF16)
        qof[a] = jnp.where(yl == 0, qx, q)
    qs[...] = jnp.where(low, qof[0], pltpu.roll(qof[1], 64, 1)).astype(BF16)
    qcopy = rc(qs, qr, qsem, qrsem, ysw)
    qcopy.start()
    for a in (a0, a1):
        kcopy(a).wait_recv()
    for way in (0, 1):
        ring(way, 1, z, 1).start()
    mst[...] = jnp.full_like(mst, -1e30)
    acc[...] = jnp.zeros_like(acc)
    qcopy.wait_recv()
    qf = qr[...].astype(F32)
    qb[512:768, :] = jnp.where(low, qf, 0.0).astype(BF16)
    qb[768:1024, :] = jnp.where(low, pltpu.roll(qf, 64, 1), 0.0).astype(BF16)

    def step(t, carry):
        i = t - 1
        z_r, g_r, z_l, g_l = slots(i)

        @pl.when(t >= 1)
        def _():
            ring(0, i, z_r, g_r).wait_recv()

            @pl.when(i <= 4)
            def _():
                ring(0, i + 2, z_r, g_r).start()

            ring(1, i, z_l, g_l).wait_recv()

            @pl.when(i <= 3)
            def _():
                ring(1, i + 2, z_l, g_l).start()

            @pl.when(i == 5)
            def _():
                ring(1, i + 1, z_l, g_l).start()

        kv = jnp.concatenate([kvb[z_r, g_r], kvb[z_l, g_l]], axis=0)
        lane = lax.broadcasted_iota(jnp.int32, kv.shape, 1)
        vals = jnp.where(lane < 64, jnp.ones_like(kv), kv)
        s = dot_t(qb[...], kv)
        n = s.shape[1] // 128
        old = mst[...]
        mx = s[:, :128]
        for j in range(1, n):
            mx = jnp.maximum(mx, s[:, j * 128 : (j + 1) * 128])
        new = jnp.maximum(old, jnp.max(mx, axis=1, keepdims=True))
        w = jnp.concatenate(
            [jnp.exp2(s[:, j * 128 : (j + 1) * 128] - new).astype(BF16) for j in range(n)], axis=1
        )
        acc[...] = acc[...] * jnp.exp2(old - new) + dot(w, vals)
        mst[...] = new
        return carry

    lax.fori_loop(0, 8, step, 0)

    for g in (0, 1):
        b0 = acc[g * 512 : g * 512 + 256, :]
        b1 = acc[g * 512 + 256 : g * 512 + 512, :]
        o0 = b0 / pltpu.roll(b0, 64, 1)
        o1 = b1 / pltpu.roll(b1, 64, 1)
        ao[g] = jnp.where(low, pltpu.roll(o0, 64, 1), o1).astype(BF16)

    def hand(g, to):
        return rc(ao.at[g], att.at[own_f, y], fsem.at[g], arsem.at[own_f, y], to)

    @pl.when(is_src)
    def _():
        hand(1, ysw).start()
        att[own_f, y] = ao[0]

    @pl.when(is_sink)
    def _():
        hand(1, yac).start()
        hand(0, part).start()

    order = [y, yh * 2 + 1 - yl, 3 - y, (1 - yh) * 2 + yl]

    def acopy(f, j, kind, to):
        ref = att.at[f, j]
        return rc(ref, ref, asem.at[kind, j], arsem.at[f, j], to)

    def await_(f, j):
        acopy(f, j, 0, sib).wait_recv()

    for i in range(5):
        if i < 4:
            j = order[i]
            if i == 0:
                @pl.when(is_sink)
                def _():
                    await_(fp, j)
            else:
                await_(fp, j)
            acopy(fp, j, 0, xsw).start()

            @pl.when(is_src)
            def _():
                acopy(fp, j, 2, xop).start()

            acopy(fp, j, 1, sib).start()
        if i >= 1:
            await_(fs, order[i - 1])
            acopy(fs, order[i - 1], 3, sib).start()
    for j in order:
        await_(fps, j)
        await_(fss, j)

    for f in range(4):
        for p in range(2):
            c0 = f * 256 + p * 128
            b0, b1 = att[f, 2 * p], att[f, 2 * p + 1]
            lhs[0, :, c0 : c0 + 128] = jnp.concatenate([b0[:, :64], b1[:, :64]], axis=1)
            lhs[1, :, c0 : c0 + 128] = jnp.concatenate([b0[:, 64:], b1[:, 64:]], axis=1)

    def gcopy(r):
        return rc(gs.at[r], gr.at[r], gsem.at[r], grsem.at[r], part)

    for r in range(2):
        gs[r] = dot(lhs[a1, r * 128 : (r + 1) * 128, :], wobuf[...]).astype(BF16)
        gcopy(r).start()
    for r in range(2):
        mine = dot(lhs[a0, r * 128 : (r + 1) * 128, :], wobuf[...])
        gcopy(r).wait_recv()
        out[r * 128 : (r + 1) * 128, :] = (mine + gr[r].astype(F32)).astype(BF16)

    for a in (a0, a1):
        for c in range(NCH):
            for kind in (0, 1, 3):
                tcopy(tslot(a, fp, c), a, fp, kind, c, sib).wait_send()
    for i in (0, 1, 2):
        for a in (a0, a1):
            ccopy(a, i).wait_send()
    for a in (a0, a1):
        kcopy(a).wait_send()
    qcopy.wait_send()
    for way in (0, 1):
        for i in range(7):
            ring(way, i, z, 0).wait_send()
    for j in range(4):
        for kind in (0, 1, 3):
            acopy(fp, j, kind, sib).wait_send()

    @pl.when(is_src)
    def _():
        hand(1, ysw).wait_send()
        for a in (a0, a1):
            for c in range(NCH):
                tcopy(tslot(a, fp, c), a, fp, 2, c, sib).wait_send()
        for j in range(4):
            acopy(fp, j, 2, sib).wait_send()

    @pl.when(is_sink)
    def _():
        hand(1, yac).wait_send()
        hand(0, part).wait_send()
        for c in range(NCH):
            pcopy(c).wait_send()

    for r in range(2):
        gcopy(r).wait_send()


def on_device(tokens, w_query, w_key, w_value, w_out):
    dma = pltpu.SemaphoreType.DMA
    scratch = [
        pltpu.VMEM((2, 4, 256, 512), BF16),
        pltpu.VMEM((3, 2048, 256), BF16),
        pltpu.VMEM((1024, 512), BF16),
        pltpu.VMEM((2, 3, 256, 128), F32),
        pltpu.VMEM((2, 3, 256, 128), BF16),
        pltpu.VMEM((2, 3, 256, 128), BF16),
        pltpu.VMEM((2, 256, 128), BF16),
        pltpu.VMEM((8, 2, 512, 128), BF16),
        pltpu.VMEM((2, 256, 128), F32),
        pltpu.VMEM((256, 128), BF16),
        pltpu.VMEM((256, 128), BF16),
        pltpu.VMEM((1024, 128), BF16),
        pltpu.VMEM((1024, 128), F32),
        pltpu.VMEM((1024, 128), F32),
        pltpu.VMEM((2, 256, 128), BF16),
        pltpu.VMEM((4, 4, 256, 128), BF16),
        pltpu.VMEM((2, 256, 1024), BF16),
        pltpu.VMEM((2, 128, 512), BF16),
        pltpu.VMEM((2, 128, 512), BF16),
        dma((4,)), dma, dma((2, 4, NCH)), dma((2, 4, NCH)), dma((NCH,)),
        dma((2, 3)), dma((2, 3)), dma((2,)), dma((2,)), dma, dma,
        dma((2, 7)), dma((2, 7)), dma((2,)), dma((4, 4)), dma((4, 4)), dma((2,)), dma((2,)),
    ]
    return pl.pallas_call(
        kernel,
        out_shape=jax.ShapeDtypeStruct((256, 512), BF16),
        in_specs=[pl.BlockSpec(memory_space=pl.ANY)] * 5,
        out_specs=pl.BlockSpec(memory_space=pltpu.VMEM),
        scratch_shapes=scratch,
        compiler_params=pltpu.CompilerParams(
            collective_id=0, has_side_effects=True, vmem_limit_bytes=48 << 20
        ),
    )(tokens, w_query, w_key, w_value, w_out)


def solution(mesh):
    in_specs = (
        P(("seq", "row"), "col"),
        P("row", "col"),
        P("row", "col"),
        P("row", "col"),
        P("row", "col"),
    )
    out_specs = P(("seq", "row"), "col")
    return jax.shard_map(
        on_device, mesh=mesh, in_specs=in_specs, out_specs=out_specs, check_vma=False
    )
```

```python
import math

import jax
import jax.numpy as jnp
from jax import lax
from jax.experimental import pallas as pl
from jax.experimental.pallas import tpu as pltpu
from jax.sharding import PartitionSpec as P

HEAD_DIM = 64
F32 = jnp.float32
BF16 = jnp.bfloat16


def dot_t(a, b):
    return lax.dot_general(a, b, (((1,), (1,)), ((), ())), preferred_element_type=F32)


def dot(a, b):
    return jnp.dot(a, b, preferred_element_type=F32)


def kernel(
    tok, wq, wk, wv, wo, out,
    tokbuf, wbuf, wobuf, pf, cs, cr, kvo, kvb, qof, qs, qr, qb, mst, acc, ao, att, lhs,
    wsem, locsem, tsem, trsem, tsib, tsibr, csem, crsem, ksem, krsem, qsem, qrsem, rsem, rrsem,
    wosem, worsem, fsem, arsem, asib, asibr,
):
    seq, yh, col = lax.axis_index("seq"), lax.axis_index("row"), lax.axis_index("col")
    z, yl = seq // 2, seq % 2
    x, k = col // 2, col % 2
    xp = x % 2
    hx = x // 2
    y = yh * 2 + yl
    src = 1 - (hx - yh) * (hx - yh)
    is_src, is_sink = src == 1, src == 0

    def dev(seq=seq, row=yh, col=col):
        return {"seq": seq, "row": row, "col": col}

    xs = [x, x + 1 - 2 * xp, 3 - x, (x + 2) % 4]
    ys = [(yl, yh), (1 - yl, 1 - yh), (1 - yl, yh), (yl, 1 - yh)]

    def at(b, i):
        return dev(seq=z * 2 + ys[b][0], row=ys[b][1], col=xs[i] * 2 + k)

    sib = dev(col=x * 2 + 1 - k)
    part, ysw = at(1, 0), at(2, 0)
    zr = dev(seq=((z + 1) % 8) * 2 + yl)
    zl = dev(seq=((z + 7) % 8) * 2 + yl)

    def rc(s, d, ss, rs, to):
        return pltpu.make_async_remote_copy(
            src_ref=s, dst_ref=d, send_sem=ss, recv_sem=rs, device_id=to,
            device_id_type=pl.DeviceIdType.MESH,
        )

    sent = {"all": [], "src": [], "sink": []}

    def go(who, make, *args):
        make(*args).start()
        sent[who].append((make, args))

    def finish():
        for make, args in sent["all"]:
            make(*args).wait_send()

        @pl.when(is_src)
        def _():
            for make, args in sent["src"]:
                make(*args).wait_send()

        @pl.when(is_sink)
        def _():
            for make, args in sent["sink"]:
                make(*args).wait_send()

    wloads = [
        pltpu.make_async_copy(w, wbuf.at[i], wsem.at[i]) for i, w in enumerate((wq, wk, wv))
    ]
    own_half = pl.ds(pl.multiple_of(yh * 1024, 1024), 1024)
    wloads.append(pltpu.make_async_copy(wo, wobuf.at[own_half, :], wsem.at[3]))
    for w in wloads:
        w.start()
    own_f = xp * 2 + k

    def tsrc(c):
        return tok.at[pl.ds(c * 128, 128), :]

    def tslot(c, f, a):
        return tokbuf.at[c, f, pl.ds(pl.multiple_of(a * 128, 128), 128), :]

    def tload(c):
        return pltpu.make_async_copy(tsrc(c), tslot(c, own_f, yh), locsem.at[c])

    @pl.when(is_src)
    def _():
        for c in range(2):
            tload(c).start()

    barrier = pltpu.get_barrier_semaphore()
    for to in [sib, zr, zl] + [at(b, i) for b in range(4) for i in range(4) if b + i > 0]:
        pl.semaphore_signal(barrier, inc=1, device_id=to, device_id_type=pl.DeviceIdType.MESH)
    pl.semaphore_wait(barrier, 18)

    def tcopy(c, b, i):
        return rc(tsrc(c), tslot(c, own_f, yh), tsem.at[c, i], trsem.at[c, own_f, yh], at(b, i))

    def twait(c, f, a):
        slot = tslot(c, f, a)
        rc(slot, slot, tsem.at[c, 0], trsem.at[c, f, a], sib).wait_recv()

    def tsibc(c, f):
        return rc(tokbuf.at[c, f], tokbuf.at[c, f], tsib.at[c, f // 2], tsibr.at[c, f], sib)

    @pl.when(is_src)
    def _():
        for c in range(2):
            for i in (3, 1, 2):
                go("src", tcopy, c, 0, i)

    @pl.when(is_sink)
    def _():
        for c in range(2):
            for i in (3, 1, 2, 0):
                go("sink", tcopy, c, 1, i)

    def ccopy(c, i):
        return rc(cs.at[c, i], cr.at[c, i], csem.at[c, i], crsem.at[c, i], part)

    def project(c):
        for i in (1, 2, 0):
            full = dot(tokbuf[c, 0], wbuf[i, 0:512, :])
            for f in range(1, 4):
                full += dot(tokbuf[c, f], wbuf[i, f * 512 : (f + 1) * 512, :])
            lo, hi = full[:, :128], full[:, 128:]
            cs[c, i] = jnp.where(yh == 0, hi, lo).astype(BF16)
            go("all", ccopy, c, i)
            pf[c, i] = jnp.where(yh == 0, lo, hi)

    for c in range(2):
        f_other = (1 - xp) * 2 + k

        @pl.when(is_src)
        def _():
            tload(c).wait()
            twait(c, own_f, 1 - yh)

        @pl.when(is_sink)
        def _():
            for a in range(2):
                twait(c, own_f, a)

        go("all", tsibc, c, own_f)
        for a in range(2):
            twait(c, f_other, a)
        go("all", tsibc, c, f_other)
        if c == 0:
            for w in wloads:
                w.wait()
        for f in (xp * 2 + 1 - k, (1 - xp) * 2 + 1 - k):
            tsibc(c, f).wait_recv()
        project(c)

    low = lax.broadcasted_iota(jnp.int32, (256, 128), 1) < 64
    qscale = math.log2(math.e) / HEAD_DIM**0.5

    def kcopy(c):
        return rc(kvo.at[c], kvb.at[z, 1, c * 256 : c * 256 + 256, :], ksem.at[c], krsem.at[c], ysw)

    for c in range(2):
        ccopy(c, 1).wait_recv()
        ccopy(c, 2).wait_recv()
        ks = pf[c, 1] + cr[c, 1].astype(F32)
        vs = pf[c, 2] + cr[c, 2].astype(F32)
        kv0 = jnp.where(low, ks, pltpu.roll(vs, 64, 1))
        kv1 = jnp.where(low, pltpu.roll(ks, 64, 1), vs)
        kvo[c] = jnp.where(yl == 0, kv1, kv0).astype(BF16)
        go("all", kcopy, c)
        kvb[z, 0, c * 256 : c * 256 + 256, :] = jnp.where(yl == 0, kv0, kv1).astype(BF16)

    def slots(i):
        t = i + 1
        d = (t + 1) // 2
        g_r = (t + 1) % 2
        ends = t // 7 + (7 - t) // 7
        g_l = g_r + ends * (1 - 2 * g_r)
        return (z - d + 8) % 8, g_r, (z + d) % 8, g_l

    def ring(way, i, zs, g):
        ref = kvb.at[zs, g]
        return rc(ref, ref, rsem.at[way, i], rrsem.at[way, i], (zr, zl)[way])

    for way in (0, 1):
        go("all", ring, way, 0, z, 0)

    for c in range(2):
        ccopy(c, 0).wait_recv()
        q = (pf[c, 0] + cr[c, 0].astype(F32)) * qscale
        qx = pltpu.roll(q, 64, 1)
        qb[c * 256 : c * 256 + 256, :] = jnp.where(
            low, jnp.where(yl == 0, q, qx), 0.0
        ).astype(BF16)
        qof[c] = jnp.where(yl == 0, qx, q)
    qs[...] = jnp.where(low, qof[0], pltpu.roll(qof[1], 64, 1)).astype(BF16)
    qcopy = rc(qs, qr, qsem, qrsem, ysw)
    go("all", lambda: qcopy)
    for c in range(2):
        kcopy(c).wait_recv()
    for way in (0, 1):
        go("all", ring, way, 1, z, 1)
    mst[...] = jnp.full_like(mst, -1e30)
    acc[...] = jnp.zeros_like(acc)
    qcopy.wait_recv()
    qf = qr[...].astype(F32)
    qb[512:768, :] = jnp.where(low, qf, 0.0).astype(BF16)
    qb[768:1024, :] = jnp.where(low, pltpu.roll(qf, 64, 1), 0.0).astype(BF16)

    def wcopy(t):
        eighth = pl.ds(pl.multiple_of(t * 128, 128), 128)
        there = pl.ds(pl.multiple_of(yh * 1024 + t * 128, 128), 128)
        return rc(wo.at[eighth, :], wobuf.at[there, :], wosem.at[t], worsem.at[t], part)

    def step(t, carry):
        i = t - 1
        z_r, g_r, z_l, g_l = slots(i)
        wcopy(t).start()

        @pl.when(t >= 1)
        def _():
            ring(0, i, z_r, g_r).wait_recv()

            @pl.when(i <= 4)
            def _():
                ring(0, i + 2, z_r, g_r).start()

            ring(1, i, z_l, g_l).wait_recv()

            @pl.when(i <= 3)
            def _():
                ring(1, i + 2, z_l, g_l).start()

            @pl.when(i == 5)
            def _():
                ring(1, i + 1, z_l, g_l).start()

        kv = jnp.concatenate([kvb[z_r, g_r], kvb[z_l, g_l]], axis=0)
        lane = lax.broadcasted_iota(jnp.int32, kv.shape, 1)
        vals = jnp.where(lane < 64, jnp.ones_like(kv), kv)
        s = dot_t(qb[...], kv)
        n = s.shape[1] // 128
        old = mst[...]
        mx = s[:, :128]
        for j in range(1, n):
            mx = jnp.maximum(mx, s[:, j * 128 : (j + 1) * 128])
        new = jnp.maximum(old, jnp.max(mx, axis=1, keepdims=True))
        w = jnp.concatenate(
            [jnp.exp2(s[:, j * 128 : (j + 1) * 128] - new).astype(BF16) for j in range(n)], axis=1
        )
        acc[...] = acc[...] * jnp.exp2(old - new) + dot(w, vals)
        mst[...] = new
        return carry

    lax.fori_loop(0, 8, step, 0)
    for way in (0, 1):
        for i in range(2, 7):
            sent["all"].append((ring, (way, i, z, 0)))
    for t in range(8):
        sent["all"].append((wcopy, (t,)))

    low2 = lax.broadcasted_iota(jnp.int32, (128, 128), 1) < 64

    def hand(b, i):
        return rc(ao.at[b], att.at[col, y], fsem.at[b, i], arsem.at[col, y], at(b, i))

    for b in (3, 1, 2, 0):
        g, a = b // 2, ys[b][1]
        r0 = pl.multiple_of(g * 512 + a * 128, 128)
        t0 = acc[pl.ds(r0, 128), :]
        t1 = acc[pl.ds(r0 + 256, 128), :]
        o0 = t0 / pltpu.roll(t0, 64, 1)
        o1 = t1 / pltpu.roll(t1, 64, 1)
        packed = jnp.where(low2, pltpu.roll(o0, 64, 1), o1).astype(BF16)
        ao[b] = packed
        if b == 0:
            att[col, y] = packed
        for i in (3, 1, 2, 0):
            if b + i > 0:
                go("all", hand, b, i)

    def acopy(q):
        c8 = xs[q] * 2 + k
        return rc(att.at[c8], att.at[c8], asib.at[q], asibr.at[c8], sib)

    for q in range(4):
        for b in range(4):
            if q + b > 0:
                ref = att.at[xs[q] * 2 + k, ys[b][1] * 2 + ys[b][0]]
                rc(ref, ref, fsem.at[0, 0], arsem.at[xs[q] * 2 + k, ys[b][1] * 2 + ys[b][0]], sib).wait_recv()
        go("all", acopy, q)
    for t in range(8):
        there = pl.ds(pl.multiple_of((1 - yh) * 1024 + t * 128, 128), 128)
        rc(wobuf.at[there, :], wobuf.at[there, :], wosem.at[t], worsem.at[t], sib).wait_recv()

    total = None
    for q in range(4):
        c8 = xs[q] * 2 + 1 - k
        rc(att.at[c8], att.at[c8], asib.at[q], asibr.at[c8], sib).wait_recv()
        for kk in range(2):
            for p in range(2):
                b0, b1 = att[xs[q] * 2 + kk, 2 * p], att[xs[q] * 2 + kk, 2 * p + 1]
                c0 = kk * 256 + p * 128
                lhs[q, 0:128, c0 : c0 + 128] = jnp.concatenate([b0[:, :64], b1[:, :64]], axis=1)
                lhs[q, 128:256, c0 : c0 + 128] = jnp.concatenate([b0[:, 64:], b1[:, 64:]], axis=1)
        term = dot(lhs[q], wobuf[pl.ds(pl.multiple_of(xs[q] * 512, 512), 512), :])
        total = term if total is None else total + term
    out[...] = total.astype(BF16)
    finish()


def on_device(tokens, w_query, w_key, w_value, w_out):
    dma = pltpu.SemaphoreType.DMA
    scratch = [
        pltpu.VMEM((2, 4, 256, 512), BF16),
        pltpu.VMEM((3, 2048, 256), BF16),
        pltpu.VMEM((2048, 512), BF16),
        pltpu.VMEM((2, 3, 256, 128), F32),
        pltpu.VMEM((2, 3, 256, 128), BF16),
        pltpu.VMEM((2, 3, 256, 128), BF16),
        pltpu.VMEM((2, 256, 128), BF16),
        pltpu.VMEM((8, 2, 512, 128), BF16),
        pltpu.VMEM((2, 256, 128), F32),
        pltpu.VMEM((256, 128), BF16),
        pltpu.VMEM((256, 128), BF16),
        pltpu.VMEM((1024, 128), BF16),
        pltpu.VMEM((1024, 128), F32),
        pltpu.VMEM((1024, 128), F32),
        pltpu.VMEM((4, 128, 128), BF16),
        pltpu.VMEM((8, 4, 128, 128), BF16),
        pltpu.VMEM((4, 256, 512), BF16),
        dma((4,)), dma((2,)), dma((2, 4)), dma((2, 4, 2)), dma((2, 2)), dma((2, 4)),
        dma((2, 3)), dma((2, 3)), dma((2,)), dma((2,)), dma, dma, dma((2, 7)), dma((2, 7)),
        dma((8,)), dma((8,)), dma((4, 4)), dma((8, 4)), dma((4,)), dma((8,)),
    ]
    return pl.pallas_call(
        kernel,
        out_shape=jax.ShapeDtypeStruct((256, 512), BF16),
        in_specs=[pl.BlockSpec(memory_space=pl.ANY)] * 5,
        out_specs=pl.BlockSpec(memory_space=pltpu.VMEM),
        scratch_shapes=scratch,
        compiler_params=pltpu.CompilerParams(
            collective_id=0, has_side_effects=True, vmem_limit_bytes=62 << 20
        ),
    )(tokens, w_query, w_key, w_value, w_out)


def solution(mesh):
    in_specs = (
        P(("seq", "row"), "col"),
        P("row", "col"),
        P("row", "col"),
        P("row", "col"),
        P("row", "col"),
    )
    out_specs = P(("seq", "row"), "col")
    return jax.shard_map(
        on_device, mesh=mesh, in_specs=in_specs, out_specs=out_specs, check_vma=False
    )
```

```python
import math

import jax
import jax.numpy as jnp
from jax import lax
from jax.experimental import pallas as pl
from jax.experimental.pallas import tpu as pltpu
from jax.sharding import PartitionSpec as P

HEAD_DIM = 64
F32 = jnp.float32
BF16 = jnp.bfloat16


def dot_t(a, b):
    return lax.dot_general(a, b, (((1,), (1,)), ((), ())), preferred_element_type=F32)


def dot(a, b):
    return jnp.dot(a, b, preferred_element_type=F32)


def kernel(
    tok, wq, wk, wv, wo, out,
    tokbuf, wbuf, wobuf, qf, pf, ps, pr, kvb, qb, mst, acc, ao, att, lhs,
    wsem, locsem, tsem, trsem, tsib, tsibr, psem, prsem, rsem, rrsem,
    wosem, worsem, fsem, arsem, asib, asibr,
):
    seq, yh, col = lax.axis_index("seq"), lax.axis_index("row"), lax.axis_index("col")
    z, yl = seq // 2, seq % 2
    x, k = col // 2, col % 2
    xp = x % 2
    hx = x // 2
    y = yh * 2 + yl
    src = 1 - (hx - yh) * (hx - yh)
    is_src, is_sink = src == 1, src == 0

    def dev(seq=seq, row=yh, col=col):
        return {"seq": seq, "row": row, "col": col}

    xs = [x, x + 1 - 2 * xp, 3 - x, (x + 2) % 4]
    ys = [(yl, yh), (1 - yl, 1 - yh), (1 - yl, yh), (yl, 1 - yh)]

    def at(b, i):
        return dev(seq=z * 2 + ys[b][0], row=ys[b][1], col=xs[i] * 2 + k)

    sib = dev(col=x * 2 + 1 - k)
    part, ysw = at(1, 0), at(2, 0)
    zr = dev(seq=((z + 1) % 8) * 2 + yl)
    zl = dev(seq=((z + 7) % 8) * 2 + yl)

    def rc(s, d, ss, rs, to):
        return pltpu.make_async_remote_copy(
            src_ref=s, dst_ref=d, send_sem=ss, recv_sem=rs, device_id=to,
            device_id_type=pl.DeviceIdType.MESH,
        )

    sent = {"all": [], "src": [], "sink": []}

    def go(who, make, *args):
        make(*args).start()
        sent[who].append((make, args))

    def finish():
        for make, args in sent["all"]:
            make(*args).wait_send()

        @pl.when(is_src)
        def _():
            for make, args in sent["src"]:
                make(*args).wait_send()

        @pl.when(is_sink)
        def _():
            for make, args in sent["sink"]:
                make(*args).wait_send()

        for pending in sent.values():
            pending.clear()

    wloads = [
        pltpu.make_async_copy(w, wbuf.at[i], wsem.at[i]) for i, w in enumerate((wq, wk, wv))
    ]
    own_half = pl.ds(pl.multiple_of(yh * 1024, 1024), 1024)
    wloads.append(pltpu.make_async_copy(wo, wobuf.at[own_half, :], wsem.at[3]))
    for w in wloads:
        w.start()
    own_f = xp * 2 + k

    def tsrc(c):
        return tok.at[pl.ds(c * 128, 128), :]

    def tslot(c, f, a):
        return tokbuf.at[c, f, pl.ds(pl.multiple_of(a * 128, 128), 128), :]

    def tload(c):
        return pltpu.make_async_copy(tsrc(c), tslot(c, own_f, yh), locsem.at[c])

    @pl.when(is_src)
    def _():
        for c in range(2):
            tload(c).start()

    barrier = pltpu.get_barrier_semaphore()
    for to in [sib, zr, zl] + [at(b, i) for b in range(4) for i in range(4) if b + i > 0]:
        pl.semaphore_signal(barrier, inc=1, device_id=to, device_id_type=pl.DeviceIdType.MESH)
    pl.semaphore_wait(barrier, 18)

    def tcopy(c, b, i):
        return rc(tsrc(c), tslot(c, own_f, yh), tsem.at[c, i], trsem.at[c, own_f, yh], at(b, i))

    def twait(c, f, a):
        slot = tslot(c, f, a)
        rc(slot, slot, tsem.at[c, 0], trsem.at[c, f, a], sib).wait_recv()

    def tsibc(c, f, a):
        slot = tslot(c, f, a)
        return rc(slot, slot, tsib.at[c, f // 2, a], tsibr.at[c, f, a], sib)

    def tsib0(c):
        return rc(
            tsrc(c), tslot(c, own_f, yh), tsib.at[c, own_f // 2, yh], tsibr.at[c, own_f, yh], sib
        )

    @pl.when(is_src)
    def _():
        for c in range(2):
            for i in (3, 1, 2):
                go("src", tcopy, c, 0, i)
            go("src", tsib0, c)

    @pl.when(is_sink)
    def _():
        for c in range(2):
            for i in (3, 1, 2, 0):
                go("sink", tcopy, c, 1, i)
    f_other = (1 - xp) * 2 + k
    not_k = 1 - k

    def pass_on(c):
        twait(c, f_other, yh)
        go("all", tsibc, c, f_other, yh)

        @pl.when(is_src)
        def _():
            tload(c).wait()

        @pl.when(is_sink)
        def _():
            twait(c, own_f, yh)
            go("sink", tsibc, c, own_f, yh)

        for f in (own_f, f_other):
            twait(c, f, 1 - yh)
            go("all", tsibc, c, f, 1 - yh)

    def from_sib(c):
        for f in (xp * 2 + not_k, (1 - xp) * 2 + not_k):
            for a in range(2):
                slot = tslot(c, f, a)
                rc(slot, slot, tsib.at[c, 0, 0], tsibr.at[c, f, a], sib).wait_recv()

    low = lax.broadcasted_iota(jnp.int32, (256, 128), 1) < 64
    qscale = math.log2(math.e) / HEAD_DIM**0.5

    def pcopy(s, b):
        j = ys[b][1] * 2 + ys[b][0]
        return rc(ps.at[s, j], pr.at[s, b], psem.at[s, b], prsem.at[s, b], at(b, 0))

    def product(c, i):
        full = dot(tokbuf[c, 0], wbuf[i, 0:512, :])
        for f in range(1, 4):
            full += dot(tokbuf[c, f], wbuf[i, f * 512 : (f + 1) * 512, :])
        return full

    def pair_up(s, left, right):
        for h in range(2):
            lt, rt = left[:, h * 128 : h * 128 + 128], right[:, h * 128 : h * 128 + 128]
            even = jnp.where(low, lt, pltpu.roll(rt, 64, 1))
            odd = jnp.where(low, pltpu.roll(lt, 64, 1), rt)
            pf[s, 2 * h], pf[s, 2 * h + 1] = even, odd
            ps[s, 2 * h], ps[s, 2 * h + 1] = even.astype(BF16), odd.astype(BF16)
        for b in (3, 1, 2):
            go("all", pcopy, s, b)

    def whole(s, g):
        if g == 0:
            pcopy(s, 1).wait_recv()
            return pf[s, y] + pr[s, 1].astype(F32)
        pcopy(s, 2).wait_recv()
        pcopy(s, 3).wait_recv()
        return pr[s, 2].astype(F32) + pr[s, 3].astype(F32)

    def slots(i):
        t = i + 1
        d = (t + 1) // 2
        g_r = (t + 1) % 2
        ends = t // 7 + (7 - t) // 7
        g_l = g_r + ends * (1 - 2 * g_r)
        return (z - d + 8) % 8, g_r, (z + d) % 8, g_l

    def ring(way, i, zs, g):
        ref = kvb.at[zs, g]
        return rc(ref, ref, rsem.at[way, i], rrsem.at[way, i], (zr, zl)[way])

    def wcopy(t):
        return rc(
            wo.at[t * 128 : t * 128 + 128, :],
            wobuf.at[pl.ds(pl.multiple_of(yh * 1024 + t * 128, 128), 128), :],
            wosem.at[t], worsem.at[t], part,
        )

    pass_on(0)
    for w in wloads:
        w.wait()
    from_sib(0)
    pair_up(0, product(0, 1), product(0, 2))
    qf[...] = product(0, 0)
    pass_on(1)
    from_sib(1)
    pair_up(1, product(1, 1), product(1, 2))
    qfull = product(1, 0)
    for h in range(2):
        lt, rt = qf[:, h * 128 : h * 128 + 128], qfull[:, h * 128 : h * 128 + 128]
        even = jnp.where(low, lt, pltpu.roll(rt, 64, 1))
        odd = jnp.where(low, pltpu.roll(lt, 64, 1), rt)
        pf[2, 2 * h], pf[2, 2 * h + 1] = even, odd
        ps[2, 2 * h], ps[2, 2 * h + 1] = even.astype(BF16), odd.astype(BF16)
    for b in (3, 1, 2):
        go("all", pcopy, 2, b)
    mst[...] = jnp.full_like(mst, -1e30)
    acc[...] = jnp.zeros_like(acc)
    for t in range(8):
        go("all", wcopy, t)
    for g in range(2):
        for c in range(2):
            kvb[z, g, c * 256 : c * 256 + 256, :] = whole(c, g).astype(BF16)
        for way in (0, 1):
            go("all", ring, way, g, z, g)
    for g in range(2):
        q = whole(2, g) * qscale
        qb[g * 512 : g * 512 + 256, :] = jnp.where(low, q, 0.0).astype(BF16)
        qb[g * 512 + 256 : g * 512 + 512, :] = jnp.where(low, pltpu.roll(q, 64, 1), 0.0).astype(BF16)

    def step(t, carry):
        i = t - 1
        z_r, g_r, z_l, g_l = slots(i)

        @pl.when(t >= 1)
        def _():
            ring(0, i, z_r, g_r).wait_recv()

            @pl.when(i <= 4)
            def _():
                ring(0, i + 2, z_r, g_r).start()

            ring(1, i, z_l, g_l).wait_recv()

            @pl.when(i <= 3)
            def _():
                ring(1, i + 2, z_l, g_l).start()

            @pl.when(i == 5)
            def _():
                ring(1, i + 1, z_l, g_l).start()

        kv = jnp.concatenate([kvb[z_r, g_r], kvb[z_l, g_l]], axis=0)
        lane = lax.broadcasted_iota(jnp.int32, kv.shape, 1)
        vals = jnp.where(lane < 64, jnp.ones_like(kv), kv)
        s = dot_t(qb[...], kv)
        n = s.shape[1] // 128
        old = mst[...]
        mx = s[:, :128]
        for j in range(1, n):
            mx = jnp.maximum(mx, s[:, j * 128 : (j + 1) * 128])
        new = jnp.maximum(old, jnp.max(mx, axis=1, keepdims=True))
        w = jnp.concatenate(
            [jnp.exp2(s[:, j * 128 : (j + 1) * 128] - new).astype(BF16) for j in range(n)], axis=1
        )
        acc[...] = acc[...] * jnp.exp2(old - new) + dot(w, vals)
        mst[...] = new
        return carry

    lax.fori_loop(0, 8, step, 0)
    for way in (0, 1):
        for i in range(2, 7):
            sent["all"].append((ring, (way, i, z, 0)))

    early = {who: pending[:] for who, pending in sent.items()}
    for pending in sent.values():
        pending.clear()
    low2 = lax.broadcasted_iota(jnp.int32, (128, 128), 1) < 64

    def hand(b, i):
        return rc(ao.at[b], att.at[col, y], fsem.at[b, i], arsem.at[col, y], at(b, i))

    for b in (3, 1, 2, 0):
        g, a = b // 2, ys[b][1]
        r0 = pl.multiple_of(g * 512 + a * 128, 128)
        t0 = acc[pl.ds(r0, 128), :]
        t1 = acc[pl.ds(r0 + 256, 128), :]
        o0 = t0 / pltpu.roll(t0, 64, 1)
        o1 = t1 / pltpu.roll(t1, 64, 1)
        packed = jnp.where(low2, pltpu.roll(o0, 64, 1), o1).astype(BF16)
        ao[b] = packed
        if b == 0:
            att[col, y] = packed
        for i in (3, 1, 2, 0):
            if b + i > 0:
                go("all", hand, b, i)

    handed = sent["all"][:]
    for who, pending in early.items():
        sent[who][:] = pending
    finish()
    sent["all"][:] = handed

    def acopy(q):
        c8 = xs[q] * 2 + k
        return rc(att.at[c8], att.at[c8], asib.at[q], asibr.at[c8], sib)

    for q in range(4):
        for b in range(4):
            if q + b > 0:
                ref = att.at[xs[q] * 2 + k, ys[b][1] * 2 + ys[b][0]]
                rc(ref, ref, fsem.at[0, 0], arsem.at[xs[q] * 2 + k, ys[b][1] * 2 + ys[b][0]], sib).wait_recv()
        go("all", acopy, q)
    for t in range(8):
        there = pl.ds(pl.multiple_of((1 - yh) * 1024 + t * 128, 128), 128)
        rc(wobuf.at[there, :], wobuf.at[there, :], wosem.at[t], worsem.at[t], sib).wait_recv()

    total = None
    for q in range(4):
        c8 = xs[q] * 2 + 1 - k
        rc(att.at[c8], att.at[c8], asib.at[q], asibr.at[c8], sib).wait_recv()
        for kk in range(2):
            for p in range(2):
                b0, b1 = att[xs[q] * 2 + kk, 2 * p], att[xs[q] * 2 + kk, 2 * p + 1]
                c0 = kk * 256 + p * 128
                lhs[q, 0:128, c0 : c0 + 128] = jnp.concatenate([b0[:, :64], b1[:, :64]], axis=1)
                lhs[q, 128:256, c0 : c0 + 128] = jnp.concatenate([b0[:, 64:], b1[:, 64:]], axis=1)
        term = dot(lhs[q], wobuf[pl.ds(pl.multiple_of(xs[q] * 512, 512), 512), :])
        total = term if total is None else total + term
    out[...] = total.astype(BF16)
    finish()


def on_device(tokens, w_query, w_key, w_value, w_out):
    dma = pltpu.SemaphoreType.DMA
    scratch = [
        pltpu.VMEM((2, 4, 256, 512), BF16),
        pltpu.VMEM((3, 2048, 256), BF16),
        pltpu.VMEM((2048, 512), BF16),
        pltpu.VMEM((256, 256), F32),
        pltpu.VMEM((3, 4, 256, 128), F32),
        pltpu.VMEM((3, 4, 256, 128), BF16),
        pltpu.VMEM((3, 4, 256, 128), BF16),
        pltpu.VMEM((8, 2, 512, 128), BF16),
        pltpu.VMEM((1024, 128), BF16),
        pltpu.VMEM((1024, 128), F32),
        pltpu.VMEM((1024, 128), F32),
        pltpu.VMEM((4, 128, 128), BF16),
        pltpu.VMEM((8, 4, 128, 128), BF16),
        pltpu.VMEM((4, 256, 512), BF16),
        dma((4,)), dma((2,)), dma((2, 4)), dma((2, 4, 2)), dma((2, 2, 2)), dma((2, 4, 2)),
        dma((3, 4)), dma((3, 4)), dma((2, 7)), dma((2, 7)),
        dma((8,)), dma((8,)), dma((4, 4)), dma((8, 4)), dma((4,)), dma((8,)),
    ]
    return pl.pallas_call(
        kernel,
        out_shape=jax.ShapeDtypeStruct((256, 512), BF16),
        in_specs=[pl.BlockSpec(memory_space=pl.ANY)] * 5,
        out_specs=pl.BlockSpec(memory_space=pltpu.VMEM),
        scratch_shapes=scratch,
        compiler_params=pltpu.CompilerParams(
            collective_id=0, has_side_effects=True, vmem_limit_bytes=54848 << 10
        ),
    )(tokens, w_query, w_key, w_value, w_out)


def solution(mesh):
    in_specs = (
        P(("seq", "row"), "col"),
        P("row", "col"),
        P("row", "col"),
        P("row", "col"),
        P("row", "col"),
    )
    out_specs = P(("seq", "row"), "col")
    return jax.shard_map(
        on_device, mesh=mesh, in_specs=in_specs, out_specs=out_specs, check_vma=False
    )
```

```python
import math

import jax
import jax.numpy as jnp
from jax import lax
from jax.experimental import pallas as pl
from jax.experimental.pallas import tpu as pltpu
from jax.sharding import PartitionSpec as P

HEAD_DIM = 64
AHEAD = 3
F32 = jnp.float32
BF16 = jnp.bfloat16


def dot_t(a, b):
    return lax.dot_general(a, b, (((1,), (1,)), ((), ())), preferred_element_type=F32)


def dot(a, b):
    return jnp.dot(a, b, preferred_element_type=F32)


def kernel(
    tok, wq, wk, wv, wo, out,
    tokbuf, wbuf, wobuf, qf, pf, ps, pr, kvb, qb, mst, acc, ao, att, lhs,
    wsem, locsem, tsem, trsem, tsib, tsibr, psem, prsem, rsem, rrsem,
    wosem, worsem, fsem, arsem, asib, asibr,
):
    seq, yh, col = lax.axis_index("seq"), lax.axis_index("row"), lax.axis_index("col")
    z, yl = seq // 2, seq % 2
    x, k = col // 2, col % 2
    xp = x % 2
    hx = x // 2
    y = yh * 2 + yl
    src = 1 - (hx - yh) * (hx - yh)
    is_src, is_sink = src == 1, src == 0

    def dev(seq=seq, row=yh, col=col):
        return {"seq": seq, "row": row, "col": col}

    xs = [x, x + 1 - 2 * xp, 3 - x, (x + 2) % 4]
    ys = [(yl, yh), (1 - yl, 1 - yh), (1 - yl, yh), (yl, 1 - yh)]

    def at(b, i):
        return dev(seq=z * 2 + ys[b][0], row=ys[b][1], col=xs[i] * 2 + k)

    sib = dev(col=x * 2 + 1 - k)
    part, ysw = at(1, 0), at(2, 0)
    zr = dev(seq=((z + 1) % 8) * 2 + yl)
    zl = dev(seq=((z + 7) % 8) * 2 + yl)

    def rc(s, d, ss, rs, to):
        return pltpu.make_async_remote_copy(
            src_ref=s, dst_ref=d, send_sem=ss, recv_sem=rs, device_id=to,
            device_id_type=pl.DeviceIdType.MESH,
        )

    sent = {"all": [], "src": [], "sink": []}

    def go(who, make, *args):
        make(*args).start()
        sent[who].append((make, args))

    def finish():
        for make, args in sent["all"]:
            make(*args).wait_send()

        @pl.when(is_src)
        def _():
            for make, args in sent["src"]:
                make(*args).wait_send()

        @pl.when(is_sink)
        def _():
            for make, args in sent["sink"]:
                make(*args).wait_send()

        for pending in sent.values():
            pending.clear()

    wloads = [
        pltpu.make_async_copy(w, wbuf.at[i], wsem.at[i]) for i, w in enumerate((wq, wk, wv))
    ]
    own_half = pl.ds(pl.multiple_of(yh * 1024, 1024), 1024)
    wloads.append(pltpu.make_async_copy(wo, wobuf.at[own_half, :], wsem.at[3]))
    for w in wloads:
        w.start()
    own_f = xp * 2 + k

    def tsrc(c):
        return tok.at[pl.ds(c * 128, 128), :]

    def tslot(c, f, a):
        return tokbuf.at[c, f, pl.ds(pl.multiple_of(a * 128, 128), 128), :]

    def tload(c):
        return pltpu.make_async_copy(tsrc(c), tslot(c, own_f, yh), locsem.at[c])

    @pl.when(is_src)
    def _():
        for c in range(2):
            tload(c).start()

    barrier = pltpu.get_barrier_semaphore()
    for to in [sib, zr, zl] + [at(b, i) for b in range(4) for i in range(4) if b + i > 0]:
        pl.semaphore_signal(barrier, inc=1, device_id=to, device_id_type=pl.DeviceIdType.MESH)
    pl.semaphore_wait(barrier, 18)

    def tcopy(c, b, i):
        return rc(tsrc(c), tslot(c, own_f, yh), tsem.at[c, i], trsem.at[c, own_f, yh], at(b, i))

    def twait(c, f, a):
        slot = tslot(c, f, a)
        rc(slot, slot, tsem.at[c, 0], trsem.at[c, f, a], sib).wait_recv()

    def tsibc(c, f, a):
        slot = tslot(c, f, a)
        return rc(slot, slot, tsib.at[c, f // 2, a], tsibr.at[c, f, a], sib)

    def tsib0(c):
        return rc(
            tsrc(c), tslot(c, own_f, yh), tsib.at[c, own_f // 2, yh], tsibr.at[c, own_f, yh], sib
        )

    @pl.when(is_src)
    def _():
        for c in range(2):
            for i in (3, 1, 2):
                go("src", tcopy, c, 0, i)
            go("src", tsib0, c)

    @pl.when(is_sink)
    def _():
        for c in range(2):
            for i in (3, 1, 2, 0):
                go("sink", tcopy, c, 1, i)
    f_other = (1 - xp) * 2 + k
    not_k = 1 - k

    def pass_on(c):
        twait(c, f_other, yh)
        go("all", tsibc, c, f_other, yh)

        @pl.when(is_src)
        def _():
            tload(c).wait()

        @pl.when(is_sink)
        def _():
            twait(c, own_f, yh)
            go("sink", tsibc, c, own_f, yh)

        for f in (own_f, f_other):
            twait(c, f, 1 - yh)
            go("all", tsibc, c, f, 1 - yh)

    def from_sib(c):
        for f in (xp * 2 + not_k, (1 - xp) * 2 + not_k):
            for a in range(2):
                slot = tslot(c, f, a)
                rc(slot, slot, tsib.at[c, 0, 0], tsibr.at[c, f, a], sib).wait_recv()

    low = lax.broadcasted_iota(jnp.int32, (256, 128), 1) < 64
    qscale = math.log2(math.e) / HEAD_DIM**0.5

    def pcopy(s, b):
        j = ys[b][1] * 2 + ys[b][0]
        return rc(ps.at[s, j], pr.at[s, b], psem.at[s, b], prsem.at[s, b], at(b, 0))

    def product(c, i):
        full = dot(tokbuf[c, 0], wbuf[i, 0:512, :])
        for f in range(1, 4):
            full += dot(tokbuf[c, f], wbuf[i, f * 512 : (f + 1) * 512, :])
        return full

    def pair_up(s, left, right):
        for h in range(2):
            lt, rt = left[:, h * 128 : h * 128 + 128], right[:, h * 128 : h * 128 + 128]
            even = jnp.where(low, lt, pltpu.roll(rt, 64, 1))
            odd = jnp.where(low, pltpu.roll(lt, 64, 1), rt)
            pf[s, 2 * h], pf[s, 2 * h + 1] = even, odd
            ps[s, 2 * h], ps[s, 2 * h + 1] = even.astype(BF16), odd.astype(BF16)
        for b in (3, 1, 2):
            go("all", pcopy, s, b)

    def whole(s, g):
        if g == 0:
            pcopy(s, 1).wait_recv()
            return pf[s, y] + pr[s, 1].astype(F32)
        pcopy(s, 2).wait_recv()
        pcopy(s, 3).wait_recv()
        return pr[s, 2].astype(F32) + pr[s, 3].astype(F32)

    def slots(i):
        t = i + 1
        d = (t + 1) // 2
        g_r = (t + 1) % 2
        ends = t // 7 + (7 - t) // 7
        g_l = g_r + ends * (1 - 2 * g_r)
        return (z - d + 8) % 8, g_r, (z + d) % 8, g_l

    def ring(way, i, c, zs, g):
        ref = kvb.at[zs, g, c * 256 : c * 256 + 256, :]
        return rc(ref, ref, rsem.at[way, i, c], rrsem.at[way, i, c], (zr, zl)[way])

    def wcopy(t):
        return rc(
            wo.at[t * 128 : t * 128 + 128, :],
            wobuf.at[pl.ds(pl.multiple_of(yh * 1024 + t * 128, 128), 128), :],
            wosem.at[t], worsem.at[t], part,
        )

    def when(cond):
        if isinstance(cond, bool):
            return (lambda f: f()) if cond else (lambda f: None)
        return pl.when(cond)

    def forward(c, i):
        z_r, g_r, z_l, g_l = slots(i)
        ring(0, i, c, z_r, g_r).wait_recv()

        @when(i <= 4)
        def _():
            ring(0, i + 2, c, z_r, g_r).start()

        ring(1, i, c, z_l, g_l).wait_recv()

        @when(i <= 3)
        def _():
            ring(1, i + 2, c, z_l, g_l).start()

        @when(i == 5)
        def _():
            ring(1, i + 1, c, z_l, g_l).start()

    def keys_values(c):
        for g in range(2):
            kvb[z, g, c * 256 : c * 256 + 256, :] = whole(c, g).astype(BF16)
            for way in (0, 1):
                go("all", ring, way, g, c, z, g)

    pass_on(0)
    for w in wloads:
        w.wait()
    from_sib(0)
    pair_up(0, product(0, 1), product(0, 2))
    qf[...] = product(0, 0)
    pass_on(1)
    from_sib(1)
    pair_up(1, product(1, 1), product(1, 2))
    keys_values(0)
    qfull = product(1, 0)
    for h in range(2):
        lt, rt = qf[:, h * 128 : h * 128 + 128], qfull[:, h * 128 : h * 128 + 128]
        even = jnp.where(low, lt, pltpu.roll(rt, 64, 1))
        odd = jnp.where(low, pltpu.roll(lt, 64, 1), rt)
        pf[2, 2 * h], pf[2, 2 * h + 1] = even, odd
        ps[2, 2 * h], ps[2, 2 * h + 1] = even.astype(BF16), odd.astype(BF16)
    for b in (3, 1, 2):
        go("all", pcopy, 2, b)
    mst[...] = jnp.full_like(mst, -1e30)
    acc[...] = jnp.zeros_like(acc)
    for t in range(8):
        go("all", wcopy, t)
    forward(0, 0)
    forward(0, 1)
    keys_values(1)
    forward(0, 2)
    for g in range(2):
        q = whole(2, g) * qscale
        qb[g * 512 : g * 512 + 256, :] = jnp.where(low, q, 0.0).astype(BF16)
        qb[g * 512 + 256 : g * 512 + 512, :] = jnp.where(low, pltpu.roll(q, 64, 1), 0.0).astype(BF16)

    def attend(z_r, g_r, z_l, g_l, r0, rows):
        r = slice(r0, r0 + rows)
        kv = jnp.concatenate([kvb[z_r, g_r], kvb[z_l, g_l]], axis=0)
        lane = lax.broadcasted_iota(jnp.int32, kv.shape, 1)
        vals = jnp.where(lane < 64, jnp.ones_like(kv), kv)
        s = dot_t(qb[r, :], kv)
        n = s.shape[1] // 128
        old = mst[r, :]
        mx = s[:, :128]
        for j in range(1, n):
            mx = jnp.maximum(mx, s[:, j * 128 : (j + 1) * 128])
        new = jnp.maximum(old, jnp.max(mx, axis=1, keepdims=True))
        w = jnp.concatenate(
            [jnp.exp2(s[:, j * 128 : (j + 1) * 128] - new).astype(BF16) for j in range(n)], axis=1
        )
        acc[r, :] = acc[r, :] * jnp.exp2(old - new) + dot(w, vals)
        mst[r, :] = new

    def step(t, carry):
        i = t - 1
        z_r, g_r, z_l, g_l = slots(i)

        @pl.when(t >= 1)
        def _():
            forward(1, i)

            @pl.when(i <= 6 - AHEAD)
            def _():
                forward(0, i + AHEAD)

        attend(z_r, g_r, z_l, g_l, 0, 1024)
        return carry

    lax.fori_loop(0, 7, step, 0)
    last = slots(6)
    forward(1, 6)
    for way in (0, 1):
        for i in range(2, 7):
            for c in range(2):
                sent["all"].append((ring, (way, i, c, z, 0)))

    early = {who: pending[:] for who, pending in sent.items()}
    for pending in sent.values():
        pending.clear()
    low2 = lax.broadcasted_iota(jnp.int32, (128, 128), 1) < 64

    def hand(b, i):
        return rc(ao.at[b], att.at[col, y], fsem.at[b, i], arsem.at[col, y], at(b, i))

    for b in (3, 2, 1, 0):
        if b % 2 == 1:
            attend(*last, (b // 2) * 512, 512)
        g, a = b // 2, ys[b][1]
        r0 = pl.multiple_of(g * 512 + a * 128, 128)
        t0 = acc[pl.ds(r0, 128), :]
        t1 = acc[pl.ds(r0 + 256, 128), :]
        o0 = t0 / pltpu.roll(t0, 64, 1)
        o1 = t1 / pltpu.roll(t1, 64, 1)
        packed = jnp.where(low2, pltpu.roll(o0, 64, 1), o1).astype(BF16)
        ao[b] = packed
        if b == 0:
            att[col, y] = packed
        for i in (3, 1, 2, 0):
            if b + i > 0:
                go("all", hand, b, i)

    handed = sent["all"][:]
    for who, pending in early.items():
        sent[who][:] = pending
    finish()
    sent["all"][:] = handed

    def acopy(q):
        c8 = xs[q] * 2 + k
        return rc(att.at[c8], att.at[c8], asib.at[q], asibr.at[c8], sib)

    for q in range(4):
        for b in range(4):
            if q + b > 0:
                ref = att.at[xs[q] * 2 + k, ys[b][1] * 2 + ys[b][0]]
                rc(ref, ref, fsem.at[0, 0], arsem.at[xs[q] * 2 + k, ys[b][1] * 2 + ys[b][0]], sib).wait_recv()
        go("all", acopy, q)
    for t in range(8):
        there = pl.ds(pl.multiple_of((1 - yh) * 1024 + t * 128, 128), 128)
        rc(wobuf.at[there, :], wobuf.at[there, :], wosem.at[t], worsem.at[t], sib).wait_recv()

    total = None
    for q in range(4):
        c8 = xs[q] * 2 + 1 - k
        rc(att.at[c8], att.at[c8], asib.at[q], asibr.at[c8], sib).wait_recv()
        for kk in range(2):
            for p in range(2):
                b0, b1 = att[xs[q] * 2 + kk, 2 * p], att[xs[q] * 2 + kk, 2 * p + 1]
                c0 = kk * 256 + p * 128
                lhs[q, 0:128, c0 : c0 + 128] = jnp.concatenate([b0[:, :64], b1[:, :64]], axis=1)
                lhs[q, 128:256, c0 : c0 + 128] = jnp.concatenate([b0[:, 64:], b1[:, 64:]], axis=1)
        term = dot(lhs[q], wobuf[pl.ds(pl.multiple_of(xs[q] * 512, 512), 512), :])
        total = term if total is None else total + term
    out[...] = total.astype(BF16)
    finish()


def on_device(tokens, w_query, w_key, w_value, w_out):
    dma = pltpu.SemaphoreType.DMA
    scratch = [
        pltpu.VMEM((2, 4, 256, 512), BF16),
        pltpu.VMEM((3, 2048, 256), BF16),
        pltpu.VMEM((2048, 512), BF16),
        pltpu.VMEM((256, 256), F32),
        pltpu.VMEM((3, 4, 256, 128), F32),
        pltpu.VMEM((3, 4, 256, 128), BF16),
        pltpu.VMEM((3, 4, 256, 128), BF16),
        pltpu.VMEM((8, 2, 512, 128), BF16),
        pltpu.VMEM((1024, 128), BF16),
        pltpu.VMEM((1024, 128), F32),
        pltpu.VMEM((1024, 128), F32),
        pltpu.VMEM((4, 128, 128), BF16),
        pltpu.VMEM((8, 4, 128, 128), BF16),
        pltpu.VMEM((4, 256, 512), BF16),
        dma((4,)), dma((2,)), dma((2, 4)), dma((2, 4, 2)), dma((2, 2, 2)), dma((2, 4, 2)),
        dma((3, 4)), dma((3, 4)), dma((2, 7, 2)), dma((2, 7, 2)),
        dma((8,)), dma((8,)), dma((4, 4)), dma((8, 4)), dma((4,)), dma((8,)),
    ]
    return pl.pallas_call(
        kernel,
        out_shape=jax.ShapeDtypeStruct((256, 512), BF16),
        in_specs=[pl.BlockSpec(memory_space=pl.ANY)] * 5,
        out_specs=pl.BlockSpec(memory_space=pltpu.VMEM),
        scratch_shapes=scratch,
        compiler_params=pltpu.CompilerParams(
            collective_id=0, has_side_effects=True, vmem_limit_bytes=54848 << 10
        ),
    )(tokens, w_query, w_key, w_value, w_out)


def solution(mesh):
    in_specs = (
        P(("seq", "row"), "col"),
        P("row", "col"),
        P("row", "col"),
        P("row", "col"),
        P("row", "col"),
    )
    out_specs = P(("seq", "row"), "col")
    return jax.shard_map(
        on_device, mesh=mesh, in_specs=in_specs, out_specs=out_specs, check_vma=False
    )
```

```python
import math

import jax
import jax.numpy as jnp
from jax import lax
from jax.experimental import pallas as pl
from jax.experimental.pallas import tpu as pltpu
from jax.sharding import PartitionSpec as P

HEAD_DIM = 64
AHEAD = 3
F32 = jnp.float32
BF16 = jnp.bfloat16


def dot_t(a, b):
    return lax.dot_general(a, b, (((1,), (1,)), ((), ())), preferred_element_type=F32)


def dot(a, b):
    return jnp.dot(a, b, preferred_element_type=F32)


def kernel(
    tok, wq, wk, wv, wo, out,
    tokbuf, wbuf, wobuf, qf, pf, ps, pr, kvb, qb, mst, acc, ao, att, lhs,
    wsem, locsem, tsem, trsem, tsib, tsibr, psem, prsem, rsem, rrsem,
    wosem, worsem, fsem, arsem, asib, asibr,
):
    seq, yh, col = lax.axis_index("seq"), lax.axis_index("row"), lax.axis_index("col")
    z, yl = seq // 2, seq % 2
    x, k = col // 2, col % 2
    xp = x % 2
    hx = x // 2
    y = yh * 2 + yl
    src = 1 - (hx - yh) * (hx - yh)
    is_src, is_sink = src == 1, src == 0

    def dev(seq=seq, row=yh, col=col):
        return {"seq": seq, "row": row, "col": col}

    xs = [x, x + 1 - 2 * xp, 3 - x, (x + 2) % 4]
    ys = [(yl, yh), (1 - yl, 1 - yh), (1 - yl, yh), (yl, 1 - yh)]

    def at(b, i):
        return dev(seq=z * 2 + ys[b][0], row=ys[b][1], col=xs[i] * 2 + k)

    sib = dev(col=x * 2 + 1 - k)
    part, ysw = at(1, 0), at(2, 0)
    zr = dev(seq=((z + 1) % 8) * 2 + yl)
    zl = dev(seq=((z + 7) % 8) * 2 + yl)

    def rc(s, d, ss, rs, to):
        return pltpu.make_async_remote_copy(
            src_ref=s, dst_ref=d, send_sem=ss, recv_sem=rs, device_id=to,
            device_id_type=pl.DeviceIdType.MESH,
        )

    sent = {"all": [], "src": [], "sink": []}

    def go(who, make, *args):
        make(*args).start()
        sent[who].append((make, args))

    def finish():
        for make, args in sent["all"]:
            make(*args).wait_send()

        @pl.when(is_src)
        def _():
            for make, args in sent["src"]:
                make(*args).wait_send()

        @pl.when(is_sink)
        def _():
            for make, args in sent["sink"]:
                make(*args).wait_send()

        for pending in sent.values():
            pending.clear()

    wloads = [
        pltpu.make_async_copy(w, wbuf.at[i], wsem.at[i]) for i, w in enumerate((wq, wk, wv))
    ]
    own_half = pl.ds(pl.multiple_of(yh * 1024, 1024), 1024)
    wloads.append(pltpu.make_async_copy(wo, wobuf.at[own_half, :], wsem.at[3]))
    for w in wloads:
        w.start()
    own_f = xp * 2 + k

    def tsrc(c):
        return tok.at[pl.ds(c * 128, 128), :]

    def tslot(c, f, a):
        return tokbuf.at[c, f, pl.ds(pl.multiple_of(a * 128, 128), 128), :]

    def tload(c):
        return pltpu.make_async_copy(tsrc(c), tslot(c, own_f, yh), locsem.at[c])

    @pl.when(is_src)
    def _():
        for c in range(2):
            tload(c).start()

    barrier = pltpu.get_barrier_semaphore()
    for to in [sib, zr, zl] + [at(b, i) for b in range(4) for i in range(4) if b + i > 0]:
        pl.semaphore_signal(barrier, inc=1, device_id=to, device_id_type=pl.DeviceIdType.MESH)
    pl.semaphore_wait(barrier, 18)

    def tcopy(c, b, i):
        return rc(tsrc(c), tslot(c, own_f, yh), tsem.at[c, i], trsem.at[c, own_f, yh], at(b, i))

    def twait(c, f, a):
        slot = tslot(c, f, a)
        rc(slot, slot, tsem.at[c, 0], trsem.at[c, f, a], sib).wait_recv()

    def tsibc(c, f, a):
        slot = tslot(c, f, a)
        return rc(slot, slot, tsib.at[c, f // 2, a], tsibr.at[c, f, a], sib)

    def tsib0(c):
        return rc(
            tsrc(c), tslot(c, own_f, yh), tsib.at[c, own_f // 2, yh], tsibr.at[c, own_f, yh], sib
        )

    @pl.when(is_src)
    def _():
        for c in range(2):
            for i in (3, 1, 2):
                go("src", tcopy, c, 0, i)
            go("src", tsib0, c)

    @pl.when(is_sink)
    def _():
        for c in range(2):
            for i in (3, 1, 2, 0):
                go("sink", tcopy, c, 1, i)
    f_other = (1 - xp) * 2 + k
    not_k = 1 - k

    def pass_on(c):
        twait(c, f_other, yh)
        go("all", tsibc, c, f_other, yh)

        @pl.when(is_src)
        def _():
            tload(c).wait()

        @pl.when(is_sink)
        def _():
            twait(c, own_f, yh)
            go("sink", tsibc, c, own_f, yh)

        for f in (own_f, f_other):
            twait(c, f, 1 - yh)
            go("all", tsibc, c, f, 1 - yh)

    def from_sib(c):
        for f in (xp * 2 + not_k, (1 - xp) * 2 + not_k):
            for a in range(2):
                slot = tslot(c, f, a)
                rc(slot, slot, tsib.at[c, 0, 0], tsibr.at[c, f, a], sib).wait_recv()

    low = lax.broadcasted_iota(jnp.int32, (256, 128), 1) < 64
    qscale = math.log2(math.e) / HEAD_DIM**0.5

    def pcopy(s, b):
        j = ys[b][1] * 2 + ys[b][0]
        return rc(ps.at[s, j], pr.at[s, b], psem.at[s, b], prsem.at[s, b], at(b, 0))

    def product(c, i):
        full = dot(tokbuf[c, 0], wbuf[i, 0:512, :])
        for f in range(1, 4):
            full += dot(tokbuf[c, f], wbuf[i, f * 512 : (f + 1) * 512, :])
        return full

    def pair_up(s, left, right):
        for h in range(2):
            lt, rt = left[:, h * 128 : h * 128 + 128], right[:, h * 128 : h * 128 + 128]
            even = jnp.where(low, lt, pltpu.roll(rt, 64, 1))
            odd = jnp.where(low, pltpu.roll(lt, 64, 1), rt)
            pf[s, 2 * h], pf[s, 2 * h + 1] = even, odd
            ps[s, 2 * h], ps[s, 2 * h + 1] = even.astype(BF16), odd.astype(BF16)
        for b in (3, 1, 2):
            go("all", pcopy, s, b)

    def whole(s, g):
        if g == 0:
            pcopy(s, 1).wait_recv()
            return pf[s, y] + pr[s, 1].astype(F32)
        pcopy(s, 2).wait_recv()
        pcopy(s, 3).wait_recv()
        return pr[s, 2].astype(F32) + pr[s, 3].astype(F32)

    def slots(i):
        t = i + 1
        d = (t + 1) // 2
        g_r = (t + 1) % 2
        ends = t // 7 + (7 - t) // 7
        g_l = g_r + ends * (1 - 2 * g_r)
        return (z - d + 8) % 8, g_r, (z + d) % 8, g_l

    def ring(way, i, c, zs, g):
        ref = kvb.at[zs, g, c * 256 : c * 256 + 256, :]
        return rc(ref, ref, rsem.at[way, i, c], rrsem.at[way, i, c], (zr, zl)[way])

    def wcopy(t):
        return rc(
            wo.at[t * 128 : t * 128 + 128, :],
            wobuf.at[pl.ds(pl.multiple_of(yh * 1024 + t * 128, 128), 128), :],
            wosem.at[t], worsem.at[t], part,
        )

    def when(cond):
        if isinstance(cond, bool):
            return (lambda f: f()) if cond else (lambda f: None)
        return pl.when(cond)

    def forward(c, i):
        z_r, g_r, z_l, g_l = slots(i)
        ring(0, i, c, z_r, g_r).wait_recv()

        @when(i <= 4)
        def _():
            ring(0, i + 2, c, z_r, g_r).start()

        ring(1, i, c, z_l, g_l).wait_recv()

        @when(i <= 3)
        def _():
            ring(1, i + 2, c, z_l, g_l).start()

        @when(i == 5)
        def _():
            ring(1, i + 1, c, z_l, g_l).start()

    def keys_values(c):
        for g in range(2):
            kvb[z, g, c * 256 : c * 256 + 256, :] = whole(c, g).astype(BF16)
            for way in (0, 1):
                go("all", ring, way, g, c, z, g)

    pass_on(0)
    for w in wloads:
        w.wait()
    from_sib(0)
    pair_up(0, product(0, 1), product(0, 2))
    qf[...] = product(0, 0)
    pass_on(1)
    from_sib(1)
    pair_up(1, product(1, 1), product(1, 2))
    keys_values(0)
    qfull = product(1, 0)
    for h in range(2):
        lt, rt = qf[:, h * 128 : h * 128 + 128], qfull[:, h * 128 : h * 128 + 128]
        even = jnp.where(low, lt, pltpu.roll(rt, 64, 1))
        odd = jnp.where(low, pltpu.roll(lt, 64, 1), rt)
        pf[2, 2 * h], pf[2, 2 * h + 1] = even, odd
        ps[2, 2 * h], ps[2, 2 * h + 1] = even.astype(BF16), odd.astype(BF16)
    for b in (3, 1, 2):
        go("all", pcopy, 2, b)
    mst[...] = jnp.full_like(mst, -1e30)
    acc[...] = jnp.zeros_like(acc)
    for t in range(8):
        go("all", wcopy, t)
    forward(0, 0)
    forward(0, 1)
    keys_values(1)
    forward(0, 2)
    for g in range(2):
        q = whole(2, g) * qscale
        qb[g * 512 : g * 512 + 256, :] = jnp.where(low, q, 0.0).astype(BF16)
        qb[g * 512 + 256 : g * 512 + 512, :] = jnp.where(low, pltpu.roll(q, 64, 1), 0.0).astype(BF16)

    def attend(z_r, g_r, z_l, g_l, r0, rows):
        r = slice(r0, r0 + rows)
        kv = jnp.concatenate([kvb[z_r, g_r], kvb[z_l, g_l]], axis=0)
        lane = lax.broadcasted_iota(jnp.int32, kv.shape, 1)
        vals = jnp.where(lane < 64, jnp.ones_like(kv), kv)
        s = dot_t(qb[r, :], kv)
        n = s.shape[1] // 128
        old = mst[r, :]
        mx = s[:, :128]
        for j in range(1, n):
            mx = jnp.maximum(mx, s[:, j * 128 : (j + 1) * 128])
        new = jnp.maximum(old, jnp.max(mx, axis=1, keepdims=True))
        w = jnp.concatenate(
            [jnp.exp2(s[:, j * 128 : (j + 1) * 128] - new).astype(BF16) for j in range(n)], axis=1
        )
        acc[r, :] = acc[r, :] * jnp.exp2(old - new) + dot(w, vals)
        mst[r, :] = new

    def step(t, carry):
        i = t - 1
        z_r, g_r, z_l, g_l = slots(i)

        @pl.when(t >= 1)
        def _():
            forward(1, i)

            @pl.when(i <= 6 - AHEAD)
            def _():
                forward(0, i + AHEAD)

        attend(z_r, g_r, z_l, g_l, 0, 1024)
        return carry

    lax.fori_loop(0, 7, step, 0)
    last = slots(6)
    forward(1, 6)
    for way in (0, 1):
        for i in range(2, 7):
            for c in range(2):
                sent["all"].append((ring, (way, i, c, z, 0)))

    early = {who: pending[:] for who, pending in sent.items()}
    for pending in sent.values():
        pending.clear()
    low2 = lax.broadcasted_iota(jnp.int32, (128, 128), 1) < 64

    def hand(b, i):
        return rc(ao.at[b], att.at[col, y], fsem.at[b, i], arsem.at[col, y], at(b, i))

    for b in (3, 2, 1, 0):
        if b % 2 == 1:
            attend(*last, (b // 2) * 512, 512)
        g, a = b // 2, ys[b][1]
        r0 = pl.multiple_of(g * 512 + a * 128, 128)
        t0 = acc[pl.ds(r0, 128), :]
        t1 = acc[pl.ds(r0 + 256, 128), :]
        o0 = t0 / pltpu.roll(t0, 64, 1)
        o1 = t1 / pltpu.roll(t1, 64, 1)
        packed = jnp.where(low2, pltpu.roll(o0, 64, 1), o1).astype(BF16)
        ao[b] = packed
        if b == 0:
            att[col, y] = packed
        for i in (3, 1, 2, 0):
            if b + i > 0:
                go("all", hand, b, i)

    handed = sent["all"][:]
    for who, pending in early.items():
        sent[who][:] = pending
    finish()
    sent["all"][:] = handed

    def acopy(q, b):
        place = xs[q] * 2 + k, ys[b][1] * 2 + ys[b][0]
        return rc(att.at[place], att.at[place], asib.at[q, b], asibr.at[place], sib)

    for q in range(4):
        for b in range(4):
            if q + b > 0:
                place = xs[q] * 2 + k, ys[b][1] * 2 + ys[b][0]
                ref = att.at[place]
                rc(ref, ref, fsem.at[0, 0], arsem.at[place], sib).wait_recv()
            go("all", acopy, q, b)
    for t in range(8):
        there = pl.ds(pl.multiple_of((1 - yh) * 1024 + t * 128, 128), 128)
        rc(wobuf.at[there, :], wobuf.at[there, :], wosem.at[t], worsem.at[t], sib).wait_recv()

    def mix(q, core, n):
        for p in range(2):
            b0, b1 = att[xs[q] * 2 + core, 2 * p], att[xs[q] * 2 + core, 2 * p + 1]
            c0 = p * 128
            lhs[n, q, 0:128, c0 : c0 + 128] = jnp.concatenate([b0[:, :64], b1[:, :64]], axis=1)
            lhs[n, q, 128:256, c0 : c0 + 128] = jnp.concatenate([b0[:, 64:], b1[:, 64:]], axis=1)
        first = pl.multiple_of(xs[q] * 512 + core * 256, 256)
        return dot(lhs[n, q], wobuf[pl.ds(first, 256), :])

    total = mix(0, k, 0)
    for q in range(1, 4):
        total += mix(q, k, 0)
    for q in range(4):
        for b in range(4):
            place = xs[q] * 2 + 1 - k, ys[b][1] * 2 + ys[b][0]
            ref = att.at[place]
            rc(ref, ref, asib.at[q, b], asibr.at[place], sib).wait_recv()
        total += mix(q, 1 - k, 1)
    out[...] = total.astype(BF16)
    finish()


def on_device(tokens, w_query, w_key, w_value, w_out):
    dma = pltpu.SemaphoreType.DMA
    scratch = [
        pltpu.VMEM((2, 4, 256, 512), BF16),
        pltpu.VMEM((3, 2048, 256), BF16),
        pltpu.VMEM((2048, 512), BF16),
        pltpu.VMEM((256, 256), F32),
        pltpu.VMEM((3, 4, 256, 128), F32),
        pltpu.VMEM((3, 4, 256, 128), BF16),
        pltpu.VMEM((3, 4, 256, 128), BF16),
        pltpu.VMEM((8, 2, 512, 128), BF16),
        pltpu.VMEM((1024, 128), BF16),
        pltpu.VMEM((1024, 128), F32),
        pltpu.VMEM((1024, 128), F32),
        pltpu.VMEM((4, 128, 128), BF16),
        pltpu.VMEM((8, 4, 128, 128), BF16),
        pltpu.VMEM((2, 4, 256, 256), BF16),
        dma((4,)), dma((2,)), dma((2, 4)), dma((2, 4, 2)), dma((2, 2, 2)), dma((2, 4, 2)),
        dma((3, 4)), dma((3, 4)), dma((2, 7, 2)), dma((2, 7, 2)),
        dma((8,)), dma((8,)), dma((4, 4)), dma((8, 4)), dma((4, 4)), dma((8, 4)),
    ]
    return pl.pallas_call(
        kernel,
        out_shape=jax.ShapeDtypeStruct((256, 512), BF16),
        in_specs=[pl.BlockSpec(memory_space=pl.ANY)] * 5,
        out_specs=pl.BlockSpec(memory_space=pltpu.VMEM),
        scratch_shapes=scratch,
        compiler_params=pltpu.CompilerParams(
            collective_id=0, has_side_effects=True, vmem_limit_bytes=54848 << 10
        ),
    )(tokens, w_query, w_key, w_value, w_out)


def solution(mesh):
    in_specs = (
        P(("seq", "row"), "col"),
        P("row", "col"),
        P("row", "col"),
        P("row", "col"),
        P("row", "col"),
    )
    out_specs = P(("seq", "row"), "col")
    return jax.shard_map(
        on_device, mesh=mesh, in_specs=in_specs, out_specs=out_specs, check_vma=False
    )
```

```python
import math

import jax
import jax.numpy as jnp
from jax import lax
from jax.experimental import pallas as pl
from jax.experimental.pallas import tpu as pltpu
from jax.sharding import PartitionSpec as P

HEAD_DIM = 64
AHEAD = 3
F32 = jnp.float32
BF16 = jnp.bfloat16


def dot_t(a, b):
    return lax.dot_general(a, b, (((1,), (1,)), ((), ())), preferred_element_type=F32)


def dot(a, b):
    return jnp.dot(a, b, preferred_element_type=F32)


def kernel(
    tok, wq, wk, wv, wo, out,
    tokbuf, wbuf, wobuf, qf, pf, ps, pr, kvb, qb, mst, acc, ao, att, lhs,
    wsem, locsem, tsem, trsem, tsib, tsibr, psem, prsem, rsem, rrsem,
    wosem, worsem, fsem, arsem, asib, asibr,
):
    seq, yh, col = lax.axis_index("seq"), lax.axis_index("row"), lax.axis_index("col")
    z, yl = seq // 2, seq % 2
    x, k = col // 2, col % 2
    xp = x % 2
    hx = x // 2
    y = yh * 2 + yl
    src = 1 - (hx - yh) * (hx - yh)
    is_src, is_sink = src == 1, src == 0

    def dev(seq=seq, row=yh, col=col):
        return {"seq": seq, "row": row, "col": col}

    xs = [x, x + 1 - 2 * xp, 3 - x, (x + 2) % 4]
    ys = [(yl, yh), (1 - yl, 1 - yh), (1 - yl, yh), (yl, 1 - yh)]

    def at(b, i):
        return dev(seq=z * 2 + ys[b][0], row=ys[b][1], col=xs[i] * 2 + k)

    sib = dev(col=x * 2 + 1 - k)
    part, ysw = at(1, 0), at(2, 0)
    zr = dev(seq=((z + 1) % 8) * 2 + yl)
    zl = dev(seq=((z + 7) % 8) * 2 + yl)

    def rc(s, d, ss, rs, to):
        return pltpu.make_async_remote_copy(
            src_ref=s, dst_ref=d, send_sem=ss, recv_sem=rs, device_id=to,
            device_id_type=pl.DeviceIdType.MESH,
        )

    sent = {"all": [], "src": [], "sink": []}

    def go(who, make, *args):
        make(*args).start()
        sent[who].append((make, args))

    def finish():
        for make, args in sent["all"]:
            make(*args).wait_send()

        @pl.when(is_src)
        def _():
            for make, args in sent["src"]:
                make(*args).wait_send()

        @pl.when(is_sink)
        def _():
            for make, args in sent["sink"]:
                make(*args).wait_send()

        for pending in sent.values():
            pending.clear()

    wloads = [
        pltpu.make_async_copy(w, wbuf.at[i], wsem.at[i]) for i, w in enumerate((wq, wk, wv))
    ]
    own_half = pl.ds(pl.multiple_of(yh * 1024, 1024), 1024)
    wloads.append(pltpu.make_async_copy(wo, wobuf.at[own_half, :], wsem.at[3]))
    for w in wloads:
        w.start()
    own_f = xp * 2 + k

    def tsrc(c):
        return tok.at[pl.ds(c * 128, 128), :]

    def tslot(c, f, a):
        return tokbuf.at[c, f, pl.ds(pl.multiple_of(a * 128, 128), 128), :]

    def tload(c):
        return pltpu.make_async_copy(tsrc(c), tslot(c, own_f, yh), locsem.at[c])

    @pl.when(is_src)
    def _():
        for c in range(2):
            tload(c).start()

    barrier = pltpu.get_barrier_semaphore()
    for to in [sib, zr, zl] + [at(b, i) for b in range(4) for i in range(4) if b + i > 0]:
        pl.semaphore_signal(barrier, inc=1, device_id=to, device_id_type=pl.DeviceIdType.MESH)
    pl.semaphore_wait(barrier, 18)

    def tcopy(c, b, i):
        return rc(tsrc(c), tslot(c, own_f, yh), tsem.at[c, i], trsem.at[c, own_f, yh], at(b, i))

    def twait(c, f, a):
        slot = tslot(c, f, a)
        rc(slot, slot, tsem.at[c, 0], trsem.at[c, f, a], sib).wait_recv()

    def tsibc(c, f, a):
        slot = tslot(c, f, a)
        return rc(slot, slot, tsib.at[c, f // 2, a], tsibr.at[c, f, a], sib)

    def tsib0(c):
        return rc(
            tsrc(c), tslot(c, own_f, yh), tsib.at[c, own_f // 2, yh], tsibr.at[c, own_f, yh], sib
        )

    @pl.when(is_src)
    def _():
        for c in range(2):
            for i in (3, 1, 2):
                go("src", tcopy, c, 0, i)
            go("src", tsib0, c)

    @pl.when(is_sink)
    def _():
        for c in range(2):
            for i in (3, 1, 2, 0):
                go("sink", tcopy, c, 1, i)
    f_other = (1 - xp) * 2 + k
    not_k = 1 - k

    def pass_on(c):
        twait(c, f_other, yh)
        go("all", tsibc, c, f_other, yh)

        @pl.when(is_src)
        def _():
            tload(c).wait()

        @pl.when(is_sink)
        def _():
            twait(c, own_f, yh)
            go("sink", tsibc, c, own_f, yh)

        for f in (own_f, f_other):
            twait(c, f, 1 - yh)
            go("all", tsibc, c, f, 1 - yh)

    def from_sib(c):
        for f in (xp * 2 + not_k, (1 - xp) * 2 + not_k):
            for a in range(2):
                slot = tslot(c, f, a)
                rc(slot, slot, tsib.at[c, 0, 0], tsibr.at[c, f, a], sib).wait_recv()

    low = lax.broadcasted_iota(jnp.int32, (256, 128), 1) < 64
    qscale = math.log2(math.e) / HEAD_DIM**0.5

    def pcopy(s, b):
        j = ys[b][1] * 2 + ys[b][0]
        return rc(ps.at[s, j], pr.at[s, b], psem.at[s, b], prsem.at[s, b], at(b, 0))

    def product(c, i):
        full = dot(tokbuf[c, 0], wbuf[i, 0:512, :])
        for f in range(1, 4):
            full += dot(tokbuf[c, f], wbuf[i, f * 512 : (f + 1) * 512, :])
        return full

    def pair_up(s, left, right):
        for h in range(2):
            lt, rt = left[:, h * 128 : h * 128 + 128], right[:, h * 128 : h * 128 + 128]
            even = jnp.where(low, lt, pltpu.roll(rt, 64, 1))
            odd = jnp.where(low, pltpu.roll(lt, 64, 1), rt)
            pf[s, 2 * h], pf[s, 2 * h + 1] = even, odd
            ps[s, 2 * h], ps[s, 2 * h + 1] = even.astype(BF16), odd.astype(BF16)
        for b in (3, 1, 2):
            go("all", pcopy, s, b)

    def whole(s, g):
        if g == 0:
            pcopy(s, 1).wait_recv()
            return pf[s, y] + pr[s, 1].astype(F32)
        pcopy(s, 2).wait_recv()
        pcopy(s, 3).wait_recv()
        return pr[s, 2].astype(F32) + pr[s, 3].astype(F32)

    def slots(i):
        t = i + 1
        d = (t + 1) // 2
        g_r = (t + 1) % 2
        ends = t // 7 + (7 - t) // 7
        g_l = g_r + ends * (1 - 2 * g_r)
        return (z - d + 8) % 8, g_r, (z + d) % 8, g_l

    def ring(way, i, c, zs, g):
        ref = kvb.at[zs, g, c * 256 : c * 256 + 256, :]
        return rc(ref, ref, rsem.at[way, i, c], rrsem.at[way, i, c], (zr, zl)[way])

    def wcopy(t):
        return rc(
            wo.at[t * 128 : t * 128 + 128, :],
            wobuf.at[pl.ds(pl.multiple_of(yh * 1024 + t * 128, 128), 128), :],
            wosem.at[t], worsem.at[t], part,
        )

    def when(cond):
        if isinstance(cond, bool):
            return (lambda f: f()) if cond else (lambda f: None)
        return pl.when(cond)

    def forward(c, i):
        z_r, g_r, z_l, g_l = slots(i)
        ring(0, i, c, z_r, g_r).wait_recv()

        @when(i <= 4)
        def _():
            ring(0, i + 2, c, z_r, g_r).start()

        ring(1, i, c, z_l, g_l).wait_recv()

        @when(i <= 3)
        def _():
            ring(1, i + 2, c, z_l, g_l).start()

        @when(i == 5)
        def _():
            ring(1, i + 1, c, z_l, g_l).start()

    def keys_values(c):
        for g in range(2):
            kvb[z, g, c * 256 : c * 256 + 256, :] = whole(c, g).astype(BF16)
            for way in (0, 1):
                go("all", ring, way, g, c, z, g)

    pass_on(0)
    for w in wloads:
        w.wait()
    from_sib(0)
    pair_up(0, product(0, 1), product(0, 2))
    qf[...] = product(0, 0)
    pass_on(1)
    from_sib(1)
    pair_up(1, product(1, 1), product(1, 2))
    keys_values(0)
    qfull = product(1, 0)
    for h in range(2):
        lt, rt = qf[:, h * 128 : h * 128 + 128], qfull[:, h * 128 : h * 128 + 128]
        even = jnp.where(low, lt, pltpu.roll(rt, 64, 1))
        odd = jnp.where(low, pltpu.roll(lt, 64, 1), rt)
        pf[2, 2 * h], pf[2, 2 * h + 1] = even, odd
        ps[2, 2 * h], ps[2, 2 * h + 1] = even.astype(BF16), odd.astype(BF16)
    for b in (3, 1, 2):
        go("all", pcopy, 2, b)
    mst[...] = jnp.full_like(mst, -1e30)
    acc[...] = jnp.zeros_like(acc)
    for t in range(4):
        go("all", wcopy, t)
    forward(0, 0)
    forward(0, 1)
    keys_values(1)
    forward(0, 2)
    for g in range(2):
        q = whole(2, g) * qscale
        qb[g * 512 : g * 512 + 256, :] = jnp.where(low, q, 0.0).astype(BF16)
        qb[g * 512 + 256 : g * 512 + 512, :] = jnp.where(low, pltpu.roll(q, 64, 1), 0.0).astype(BF16)

    for t in range(4, 8):
        go("all", wcopy, t)

    def attend(z_r, g_r, z_l, g_l, r0, rows):
        r = slice(r0, r0 + rows)
        kv = jnp.concatenate([kvb[z_r, g_r], kvb[z_l, g_l]], axis=0)
        lane = lax.broadcasted_iota(jnp.int32, kv.shape, 1)
        vals = jnp.where(lane < 64, jnp.ones_like(kv), kv)
        s = dot_t(qb[r, :], kv)
        n = s.shape[1] // 128
        old = mst[r, :]
        mx = s[:, :128]
        for j in range(1, n):
            mx = jnp.maximum(mx, s[:, j * 128 : (j + 1) * 128])
        new = jnp.maximum(old, jnp.max(mx, axis=1, keepdims=True))
        w = jnp.concatenate(
            [jnp.exp2(s[:, j * 128 : (j + 1) * 128] - new).astype(BF16) for j in range(n)], axis=1
        )
        acc[r, :] = acc[r, :] * jnp.exp2(old - new) + dot(w, vals)
        mst[r, :] = new

    def step(t, carry):
        i = t - 1
        z_r, g_r, z_l, g_l = slots(i)

        @pl.when(t >= 1)
        def _():
            forward(1, i)

            @pl.when(i <= 6 - AHEAD)
            def _():
                forward(0, i + AHEAD)

        attend(z_r, g_r, z_l, g_l, 0, 1024)
        return carry

    lax.fori_loop(0, 7, step, 0)
    last = slots(6)
    forward(1, 6)
    for way in (0, 1):
        for i in range(2, 7):
            for c in range(2):
                sent["all"].append((ring, (way, i, c, z, 0)))

    early = {who: pending[:] for who, pending in sent.items()}
    for pending in sent.values():
        pending.clear()
    low2 = lax.broadcasted_iota(jnp.int32, (128, 128), 1) < 64

    def hand(b, i):
        return rc(ao.at[b], att.at[col, y], fsem.at[b, i], arsem.at[col, y], at(b, i))

    for b in (3, 2, 1, 0):
        if b % 2 == 1:
            attend(*last, (b // 2) * 512, 512)
        g, a = b // 2, ys[b][1]
        r0 = pl.multiple_of(g * 512 + a * 128, 128)
        t0 = acc[pl.ds(r0, 128), :]
        t1 = acc[pl.ds(r0 + 256, 128), :]
        o0 = t0 / pltpu.roll(t0, 64, 1)
        o1 = t1 / pltpu.roll(t1, 64, 1)
        packed = jnp.where(low2, pltpu.roll(o0, 64, 1), o1).astype(BF16)
        ao[b] = packed
        if b == 0:
            att[col, y] = packed
        for i in (3, 1, 2, 0):
            if b + i > 0:
                go("all", hand, b, i)

    handed = sent["all"][:]
    for who, pending in early.items():
        sent[who][:] = pending
    finish()
    sent["all"][:] = handed

    def acopy(q):
        c8 = xs[q] * 2 + k
        return rc(att.at[c8], att.at[c8], asib.at[q], asibr.at[c8], sib)

    for q in range(4):
        for b in range(4):
            if q + b > 0:
                ref = att.at[xs[q] * 2 + k, ys[b][1] * 2 + ys[b][0]]
                rc(ref, ref, fsem.at[0, 0], arsem.at[xs[q] * 2 + k, ys[b][1] * 2 + ys[b][0]], sib).wait_recv()
        go("all", acopy, q)
    for t in range(8):
        there = pl.ds(pl.multiple_of((1 - yh) * 1024 + t * 128, 128), 128)
        rc(wobuf.at[there, :], wobuf.at[there, :], wosem.at[t], worsem.at[t], sib).wait_recv()

    total = None
    for q in range(4):
        c8 = xs[q] * 2 + 1 - k
        rc(att.at[c8], att.at[c8], asib.at[q], asibr.at[c8], sib).wait_recv()
        for kk in range(2):
            for p in range(2):
                b0, b1 = att[xs[q] * 2 + kk, 2 * p], att[xs[q] * 2 + kk, 2 * p + 1]
                c0 = kk * 256 + p * 128
                lhs[q, 0:128, c0 : c0 + 128] = jnp.concatenate([b0[:, :64], b1[:, :64]], axis=1)
                lhs[q, 128:256, c0 : c0 + 128] = jnp.concatenate([b0[:, 64:], b1[:, 64:]], axis=1)
        term = dot(lhs[q], wobuf[pl.ds(pl.multiple_of(xs[q] * 512, 512), 512), :])
        total = term if total is None else total + term
    out[...] = total.astype(BF16)
    finish()


def on_device(tokens, w_query, w_key, w_value, w_out):
    dma = pltpu.SemaphoreType.DMA
    scratch = [
        pltpu.VMEM((2, 4, 256, 512), BF16),
        pltpu.VMEM((3, 2048, 256), BF16),
        pltpu.VMEM((2048, 512), BF16),
        pltpu.VMEM((256, 256), F32),
        pltpu.VMEM((3, 4, 256, 128), F32),
        pltpu.VMEM((3, 4, 256, 128), BF16),
        pltpu.VMEM((3, 4, 256, 128), BF16),
        pltpu.VMEM((8, 2, 512, 128), BF16),
        pltpu.VMEM((1024, 128), BF16),
        pltpu.VMEM((1024, 128), F32),
        pltpu.VMEM((1024, 128), F32),
        pltpu.VMEM((4, 128, 128), BF16),
        pltpu.VMEM((8, 4, 128, 128), BF16),
        pltpu.VMEM((4, 256, 512), BF16),
        dma((4,)), dma((2,)), dma((2, 4)), dma((2, 4, 2)), dma((2, 2, 2)), dma((2, 4, 2)),
        dma((3, 4)), dma((3, 4)), dma((2, 7, 2)), dma((2, 7, 2)),
        dma((8,)), dma((8,)), dma((4, 4)), dma((8, 4)), dma((4,)), dma((8,)),
    ]
    return pl.pallas_call(
        kernel,
        out_shape=jax.ShapeDtypeStruct((256, 512), BF16),
        in_specs=[pl.BlockSpec(memory_space=pl.ANY)] * 5,
        out_specs=pl.BlockSpec(memory_space=pltpu.VMEM),
        scratch_shapes=scratch,
        compiler_params=pltpu.CompilerParams(
            collective_id=0, has_side_effects=True, vmem_limit_bytes=54848 << 10
        ),
    )(tokens, w_query, w_key, w_value, w_out)


def solution(mesh):
    in_specs = (
        P(("seq", "row"), "col"),
        P("row", "col"),
        P("row", "col"),
        P("row", "col"),
        P("row", "col"),
    )
    out_specs = P(("seq", "row"), "col")
    return jax.shard_map(
        on_device, mesh=mesh, in_specs=in_specs, out_specs=out_specs, check_vma=False
    )
```
